512 devices in a mesh: row: 32 (over x_hi, z), col: 16 (over x_lo, y, core).
Axes of the slice: x: 4 (x_hi: 2, x_lo: 2; x = x_hi * 2 + x_lo), y: 4, z: 16, core: 2. Of those that a mesh axis runs over, the one named last changes fastest.
Arguments:
- start_block: float32 [1024, 32, 128], P(('col', 'row')), may hold values from -34 to 34
- tile_values: bfloat16 [32, 16, 48, 128, 128], P('row', 'col'), may hold values from -0.078125 to 0.078125
- tile_rows: int32 [32, 16, 48], P('row', 'col'), may hold values from 0 to 31, as said below
- tile_columns: int32 [32, 16, 48], P('row', 'col'), may hold values from 0 to 63, as said below
- diagonal_blocks: bfloat16 [1024, 128, 128], P(('col', 'row')), may hold values from -0.078125 to 0.078125
Outputs:
- basis_block: float32 [1024, 32, 128], P(('col', 'row'))
- alpha_blocks: float32 [2, 32, 32], replicated
- beta_blocks: float32 [2, 32, 32], replicated
The draws below stay inside these ranges and needn't reach their ends.
Inputs may be any that keep to these rules, and one draw needn't show every extreme that they name: `tile_rows`: each grid position lists 48 distinct stored blocks, ordered by local block row and then local block column, and every local block row holds at least one. Write a block's global index as s * 2 + p with segment s and place p; a block of segments a != b and places p, q is stored exactly when (a < b) equals (p + q even); within one segment exactly when p < q. `tile_columns`: local block columns, obeying the storage rule stated for tile_rows.
All inputs are finite; a program needn't handle non-finite values.
Results may differ from the reference program's by a relative error of at most 0.006.
Values may be sent and summed in bfloat16 or wider, within the bound.
No kernel may reach another device: no remote copies, remote signals or barrier semaphores. Data moves between devices by JAX's collectives and lax.ppermute only.
A program may use at most 64 MiB of HBM per device.

```python
import math
import jax
import jax.numpy as jnp
from jax import lax

K = 32
BS = 128
BLK_DEV = 2
HALF_ROW = 24
ITERS = 2
NBLOCKS = 1024
NODES = 131072
TILES_DEV = 48
N_ROW = 32
N_COL = 16


def draw_start_block(key, part):
    key = jax.random.fold_in(key, 7)
    key_noise, key_rows, key_columns = jax.random.split(key, 3)
    full_shape = (NBLOCKS, K, BS)
    noise_values = jax.random.normal(key_noise, full_shape, jnp.float32)
    noise_values = jnp.clip(noise_values, -4.0, 4.0)
    position = jnp.arange(NBLOCKS, dtype=jnp.float32)[:, None, None] / NBLOCKS
    rising = jnp.exp(jnp.log(3.0) * position)
    row_scale = jnp.exp(jax.random.uniform(key_rows, (NBLOCKS, 1, BS), jnp.float32) * jnp.log(10.0 / 3.0))
    column_scale = jnp.exp(jax.random.uniform(key_columns, (1, K, 1), jnp.float32) * jnp.log(10.0 / 3.0))
    return noise_values * rising * row_scale * column_scale * 0.25


def tile_pattern(key):
    key = jax.random.fold_in(key, 5)
    row_blocks = N_COL * BLK_DEV
    column_blocks = N_ROW * BLK_DEV
    places = row_blocks * column_blocks
    place_index = jnp.arange(places, dtype=jnp.int32)
    local_row = place_index // column_blocks
    local_column = place_index % column_blocks

    def one_device(device):
        row_index = device // N_COL
        col_index = device % N_COL
        left_segment = local_row // BLK_DEV * N_ROW + row_index
        left_place = local_row % BLK_DEV
        right_segment = col_index * N_ROW + local_column // BLK_DEV
        right_place = local_column % BLK_DEV
        parity_even = (left_place + right_place) % 2 == 0
        stored = jnp.where(left_segment == right_segment, left_place < right_place, (left_segment < right_segment) == parity_even)
        device_key = jax.random.fold_in(key, device)
        raw_score = jax.random.randint(device_key, (places,), 0, 4096, dtype=jnp.int32) * places + place_index
        score_flat = jnp.where(stored, raw_score, raw_score + (1 << 30))
        score_grid = score_flat.reshape(row_blocks, column_blocks)
        row_first = (score_grid == jnp.min(score_grid, axis=1, keepdims=True)).reshape(-1)
        final_score = jnp.where(row_first, place_index - (1 << 30), score_flat)
        ranking = jnp.argsort(final_score)
        chosen = jnp.sort(ranking[:TILES_DEV]).astype(jnp.int32)
        return (chosen // column_blocks, chosen % column_blocks)
    devices = jnp.arange(N_ROW * N_COL, dtype=jnp.int32)
    rows_drawn, columns_drawn = jax.vmap(one_device)(devices)
    return (rows_drawn.reshape(N_ROW, N_COL, TILES_DEV), columns_drawn.reshape(N_ROW, N_COL, TILES_DEV))


def draw_tile_rows(key, part):
    return tile_pattern(key)[0]


def draw_tile_columns(key, part):
    return tile_pattern(key)[1]


def block_levels(rng, shape, cuts, low, largest):
    factor_of, own = 1.0, jax.random.fold_in(rng, 6)
    for dim, parts in cuts:
        draws = jnp.exp(jax.random.uniform(jax.random.fold_in(own, dim), (parts,), jnp.float32, low / len(cuts), largest / len(cuts)))
        factor_of = factor_of * jnp.repeat(draws, shape[dim] // parts).reshape([-1 if axis == dim else 1 for axis in range(len(shape))])
    return factor_of


def normal_values(key, shape, spread, most, shards=(), kind=jnp.bfloat16):
    gain = block_levels(key, shape, shards, -0.22, 0.18) if shards else 1.0
    drawn = jax.random.normal(key, shape, jnp.float32) * spread * gain
    return jnp.minimum(jnp.maximum(drawn, -most), most).astype(kind)


def setup_inputs(seed: int = 0) -> dict:
    key_of = jax.random.split(jax.random.key(seed), 6)
    return {
        "start_block": draw_start_block(jax.random.fold_in(key_of[5], 71), 0),
        "tile_values": normal_values(key_of[1], (N_ROW, N_COL, TILES_DEV, BS, BS), (2 * HALF_ROW * BS) ** -0.5, 0.078125, ((0, 32), (1, 16))),
        "tile_rows": draw_tile_rows(jax.random.fold_in(key_of[5], 71), 0),
        "tile_columns": draw_tile_columns(jax.random.fold_in(key_of[5], 71), 0),
        "diagonal_blocks": normal_values(key_of[4], (NBLOCKS, BS, BS), (2 * HALF_ROW * BS) ** -0.5, 0.078125, ((0, 512),)),
    }


highest = lax.Precision.HIGHEST

def block_index(tile_rows, tile_columns):
    row_index = jnp.arange(N_ROW, dtype=jnp.int32)[:, None, None]
    col_index = jnp.arange(N_COL, dtype=jnp.int32)[None, :, None]
    left_ids = (tile_rows // BLK_DEV * N_ROW + row_index) * BLK_DEV + tile_rows % BLK_DEV
    right_ids = (col_index * N_ROW + tile_columns // BLK_DEV) * BLK_DEV + tile_columns % BLK_DEV
    left_ids = left_ids.reshape(N_ROW * N_COL, TILES_DEV).astype(jnp.int32)
    right_ids = right_ids.reshape(N_ROW * N_COL, TILES_DEV).astype(jnp.int32)
    return (left_ids, right_ids)

def apply_operator(narrow, tile_values, left_ids, right_ids, diagonal_blocks):
    narrow = lax.optimization_barrier(narrow)
    blocks = narrow.astype(jnp.float32)
    tile_sets = tile_values.reshape(N_ROW * N_COL, TILES_DEV, BS, BS)

    def add_device(running, device_data):
        tile_set, left_rows, right_cols = device_data
        tile_float = tile_set.astype(jnp.float32)
        upper_part = jnp.einsum('tkj,tij->tki', blocks[right_cols], tile_float, precision=highest)
        lower_part = jnp.einsum('tki,tij->tkj', blocks[left_rows], tile_float, precision=highest)
        running = running.at[left_rows].add(upper_part).at[right_cols].add(lower_part)
        return (running, None)
    running, _ = lax.scan(add_device, jnp.zeros(blocks.shape, jnp.float32), (tile_sets, left_ids, right_ids))
    diag_float = diagonal_blocks.astype(jnp.float32)
    diagonal = 0.5 * (jnp.einsum('bkj,bij->bki', blocks, diag_float, precision=highest) + jnp.einsum('bki,bij->bkj', blocks, diag_float, precision=highest))
    return running + diagonal

def gram_of(left_side, right_side):
    return jnp.einsum('bkn,bln->kl', left_side, right_side, precision=highest)

def apply_inverse(factor, vectors):
    inverse = jax.scipy.linalg.solve_triangular(factor, jnp.eye(factor.shape[0], dtype=jnp.float32), lower=True)
    return jnp.einsum('kl,bln->bkn', inverse, vectors, precision=highest)

def reference(start_block, tile_values, tile_rows, tile_columns, diagonal_blocks):
    left_ids, right_ids = block_index(tile_rows, tile_columns)
    gram_sum = gram_of(start_block, start_block)
    factor = jnp.linalg.cholesky(gram_sum)
    current = apply_inverse(factor, start_block)
    previous = current
    alpha_list = []
    beta_list = []
    for iteration in range(ITERS):
        image_block = apply_operator(current.astype(jnp.bfloat16), tile_values, left_ids, right_ids, diagonal_blocks)
        if iteration > 0:
            image_block = image_block - jnp.einsum('lk,bln->bkn', factor, previous, precision=highest)
        projection = gram_of(current, image_block)
        residual = image_block - jnp.einsum('lk,bln->bkn', projection, current, precision=highest)
        gram_sum = gram_of(residual, residual)
        factor = jnp.linalg.cholesky(gram_sum)
        previous = current
        current = apply_inverse(factor, residual)
        alpha_list.append(projection)
        beta_list.append(factor)
    return (current * math.sqrt(NODES), jnp.stack(alpha_list), jnp.stack(beta_list))
```

```python
import math

import jax
import jax.numpy as jnp
from jax import lax
from jax.sharding import PartitionSpec as P

highest = lax.Precision.HIGHEST


def gram_of(left_side, right_side):
    return jnp.einsum("bkn,bln->kl", left_side, right_side, precision=highest)


def mix(matrix, vectors):
    return jnp.einsum("kl,bln->bkn", matrix, vectors, precision=highest)


def dot(left_side, right_side):
    return jnp.dot(left_side, right_side, precision=highest)


def swap(parts, axis):
    return lax.all_to_all(parts, axis, 0, 0, tiled=True)


def gather(block, axis):
    size = lax.axis_size(axis)
    slab = jnp.broadcast_to(block[None], (size, *block.shape))
    return swap(slab, axis)


def sum_all(stacked):
    partial = jnp.sum(gather(stacked, "col"), axis=0)
    return jnp.sum(gather(partial, "row"), axis=0)


def block_sums(selected, products, row_count):
    targets = jnp.arange(row_count, dtype=jnp.int32)
    picker = (targets[:, None] == selected[None, :]).astype(jnp.float32)
    return jnp.dot(picker, products, precision=highest)


def scatter(sums, axis, shape):
    parts = sums.astype(jnp.bfloat16).reshape(lax.axis_size(axis), *shape)
    return jnp.sum(swap(parts, axis).astype(jnp.float32), axis=0)


def apply_operator(vectors, tile_set, row_list, column_list, diagonal_blocks):
    narrow = vectors.astype(jnp.bfloat16)
    shape = narrow.shape
    own_blocks = shape[0]
    count_tiles = tile_set.shape[0]
    column_slab = gather(narrow, "row").reshape(-1, *shape[1:])
    row_slab = gather(narrow, "col").reshape(-1, *shape[1:])
    lower_part = jnp.einsum(
        "tki,tij->tkj", row_slab[row_list], tile_set, preferred_element_type=jnp.float32
    ).reshape(count_tiles, -1)
    from_columns = scatter(
        block_sums(column_list, lower_part, own_blocks * lax.axis_size("row")), "row", shape
    )
    upper_part = jnp.einsum(
        "tkj,tij->tki", column_slab[column_list], tile_set, preferred_element_type=jnp.float32
    ).reshape(count_tiles, -1)
    from_rows = scatter(
        block_sums(row_list, upper_part, own_blocks * lax.axis_size("col")), "col", shape
    )
    diagonal = 0.5 * (
        jnp.einsum("bkj,bij->bki", narrow, diagonal_blocks, preferred_element_type=jnp.float32)
        + jnp.einsum("bki,bij->bkj", narrow, diagonal_blocks, preferred_element_type=jnp.float32)
    )
    return from_rows + from_columns + diagonal


def factor_of(gram):
    factor = jnp.linalg.cholesky(gram)
    inverse = jax.scipy.linalg.solve_triangular(
        factor, jnp.eye(factor.shape[0], dtype=jnp.float32), lower=True
    )
    return factor, inverse


def local(start_block, tile_values, tile_rows, tile_columns, diagonal_blocks):
    matrix = (tile_values[0, 0], tile_rows[0, 0], tile_columns[0, 0], diagonal_blocks)
    first = apply_operator(start_block, *matrix)
    sums = sum_all(
        jnp.stack(
            [gram_of(start_block, start_block), gram_of(start_block, first), gram_of(first, first)]
        )
    )
    second = apply_operator(first, *matrix)
    _, inverse_start = factor_of(sums[0])
    alpha_first = dot(dot(inverse_start, sums[1]), inverse_start.T)
    image_gram = dot(dot(inverse_start, sums[2]), inverse_start.T)
    beta_first, inverse_first = factor_of(image_gram - dot(alpha_first.T, alpha_first))
    basis_start = mix(inverse_start, start_block)
    image_start = mix(inverse_start, first)
    basis_first = mix(inverse_first, image_start - mix(alpha_first.T, basis_start))
    moved = mix(inverse_start, second) - mix(alpha_first.T, image_start)
    image_first = mix(inverse_first, moved) - mix(beta_first.T, basis_start)
    last = sum_all(jnp.stack([gram_of(basis_first, image_first), gram_of(image_first, image_first)]))
    alpha_last = last[0]
    beta_last, inverse_last = factor_of(last[1] - dot(alpha_last.T, alpha_last))
    basis_last = mix(inverse_last, image_first - mix(alpha_last.T, basis_first))
    scaling = math.sqrt(
        start_block.shape[0] * start_block.shape[2] * lax.axis_size("row") * lax.axis_size("col")
    )
    return (
        basis_last * scaling,
        jnp.stack([alpha_first, alpha_last]),
        jnp.stack([beta_first, beta_last]),
    )


def solution(mesh):
    placed = (
        P(("col", "row"), None, None),
        P("row", "col", None, None, None),
        P("row", "col", None),
        P("row", "col", None),
        P(("col", "row"), None, None),
    )
    return jax.shard_map(
        local,
        mesh=mesh,
        in_specs=placed,
        out_specs=(P(("col", "row"), None, None), P(), P()),
        check_vma=False,
    )
```

```python
import math

import jax
import jax.numpy as jnp
from jax import lax
from jax.sharding import PartitionSpec as P

highest = lax.Precision.HIGHEST


def gram_of(left_side, right_side):
    return jnp.einsum("bkn,bln->kl", left_side, right_side, precision=highest)


def mix(matrix, vectors):
    return jnp.einsum("kl,bln->bkn", matrix, vectors, precision=highest)


def dot(left_side, right_side):
    return jnp.dot(left_side, right_side, precision=highest)


def swap(parts, axis):
    return lax.all_to_all(parts, axis, 0, 0, tiled=True)


def copies(rows, count):
    return jnp.broadcast_to(rows[None], (count, *rows.shape))


def pack(values):
    high = lax.reduce_precision(values, 8, 7)
    rest = values - high
    middle = lax.reduce_precision(rest, 8, 7)
    terms = jnp.stack([high, middle, rest - middle], axis=-2).astype(jnp.bfloat16)
    widths = [(0, 0)] * (terms.ndim - 2) + [(0, 5), (0, 128 - terms.shape[-1])]
    return jnp.pad(terms, widths)


def unpack(rows, width):
    terms = rows[..., :3, :width].astype(jnp.float32)
    return terms[..., 0, :] + (terms[..., 1, :] + terms[..., 2, :])


def sum_all(stacked):
    flat = stacked.reshape(-1, 128)
    partial = jnp.sum(swap(copies(flat, lax.axis_size("col")), "col"), axis=0)
    total = jnp.sum(swap(copies(partial, lax.axis_size("row")), "row"), axis=0)
    return total.reshape(stacked.shape)


def block_sums(selected, products, row_count):
    targets = jnp.arange(row_count, dtype=jnp.int32)
    picker = (targets[:, None] == selected[None, :]).astype(jnp.float32)
    return jnp.dot(picker, products, precision=highest)


def apply_operator(vectors, grams, tile_set, row_list, column_list, diagonal_blocks):
    narrow = vectors.astype(jnp.bfloat16)
    shape = narrow.shape
    own_blocks = shape[0]
    height = shape[0] * shape[1]
    own = narrow.reshape(height, shape[2])
    rows, columns = lax.axis_size("row"), lax.axis_size("col")
    count_tiles = tile_set.shape[0]
    width = grams.size // columns

    sent = jnp.concatenate(
        [copies(own, columns), pack(grams.reshape(columns, width))], axis=1
    )
    got = swap(sent, "col")
    row_slab = got[:, :height].reshape(-1, *shape[1:])
    piece = jnp.sum(unpack(got[:, height:], width), axis=0)
    lower_part = jnp.einsum(
        "tki,tij->tkj", row_slab[row_list], tile_set, preferred_element_type=jnp.float32
    ).reshape(count_tiles, -1)
    lower = block_sums(column_list, lower_part, own_blocks * rows).astype(jnp.bfloat16)
    sent = jnp.concatenate(
        [copies(own, rows), lower.reshape(rows, height, -1), copies(pack(piece), rows)], axis=1
    )
    got = swap(sent, "row")
    column_slab = got[:, :height].reshape(-1, *shape[1:])
    from_columns = jnp.sum(got[:, height : 2 * height].astype(jnp.float32), axis=0)
    piece = jnp.sum(unpack(got[:, 2 * height :], width), axis=0)
    upper_part = jnp.einsum(
        "tkj,tij->tki", column_slab[column_list], tile_set, preferred_element_type=jnp.float32
    ).reshape(count_tiles, -1)
    upper = block_sums(row_list, upper_part, own_blocks * columns).astype(jnp.bfloat16)
    sent = jnp.concatenate(
        [upper.reshape(columns, height, -1), copies(pack(piece), columns)], axis=1
    )
    got = swap(sent, "col")
    from_rows = jnp.sum(got[:, :height].astype(jnp.float32), axis=0)
    diagonal = 0.5 * (
        jnp.einsum("bkj,bij->bki", narrow, diagonal_blocks, preferred_element_type=jnp.float32)
        + jnp.einsum("bki,bij->bkj", narrow, diagonal_blocks, preferred_element_type=jnp.float32)
    )
    image = (from_rows + from_columns).reshape(shape) + diagonal
    return image, unpack(got[:, height:], width).reshape(grams.shape)


def factor_of(gram):
    factor = jnp.linalg.cholesky(gram)
    inverse = jax.scipy.linalg.solve_triangular(
        factor, jnp.eye(factor.shape[0], dtype=jnp.float32), lower=True
    )
    return factor, inverse


def local(start_block, tile_values, tile_rows, tile_columns, diagonal_blocks):
    matrix = (tile_values[0, 0], tile_rows[0, 0], tile_columns[0, 0], diagonal_blocks)
    start_gram = gram_of(start_block, start_block)[None]
    first, start_sum = apply_operator(start_block, start_gram, *matrix)
    first_grams = jnp.stack([gram_of(start_block, first), gram_of(first, first)])
    second, sums = apply_operator(first, first_grams, *matrix)
    _, inverse_start = factor_of(start_sum[0])
    alpha_first = dot(dot(inverse_start, sums[0]), inverse_start.T)
    image_gram = dot(dot(inverse_start, sums[1]), inverse_start.T)
    beta_first, inverse_first = factor_of(image_gram - dot(alpha_first.T, alpha_first))
    basis_start = mix(inverse_start, start_block)
    image_start = mix(inverse_start, first)
    basis_first = mix(inverse_first, image_start - mix(alpha_first.T, basis_start))
    moved = mix(inverse_start, second) - mix(alpha_first.T, image_start)
    image_first = mix(inverse_first, moved) - mix(beta_first.T, basis_start)
    last = sum_all(jnp.stack([gram_of(basis_first, image_first), gram_of(image_first, image_first)]))
    alpha_last = last[0]
    beta_last, inverse_last = factor_of(last[1] - dot(alpha_last.T, alpha_last))
    basis_last = mix(inverse_last, image_first - mix(alpha_last.T, basis_first))
    scaling = math.sqrt(
        start_block.shape[0] * start_block.shape[2] * lax.axis_size("row") * lax.axis_size("col")
    )
    return (
        basis_last * scaling,
        jnp.stack([alpha_first, alpha_last]),
        jnp.stack([beta_first, beta_last]),
    )


def solution(mesh):
    placed = (
        P(("col", "row"), None, None),
        P("row", "col", None, None, None),
        P("row", "col", None),
        P("row", "col", None),
        P(("col", "row"), None, None),
    )
    return jax.shard_map(
        local,
        mesh=mesh,
        in_specs=placed,
        out_specs=(P(("col", "row"), None, None), P(), P()),
        check_vma=False,
    )
```

```python
import math

import jax
import jax.numpy as jnp
from jax import lax
from jax.sharding import Mesh
from jax.sharding import PartitionSpec as P

highest = lax.Precision.HIGHEST

AXES = ("x_high", "far", "near", "x_low", "y", "core")
COLUMN = ("x_low", "y", "core")
PLANE = ("x_high", *COLUMN)
DEPTH = ("far", "near")
NEAR = ("x_high", "near")
FAR = ("far",)


def gram_of(left_side, right_side):
    return jnp.einsum("bkn,bln->kl", left_side, right_side, precision=highest)


def mix(matrix, vectors):
    return jnp.einsum("kl,bln->bkn", matrix, vectors, precision=highest)


def dot(left_side, right_side):
    return jnp.dot(left_side, right_side, precision=highest)


def swap(parts, axis):
    return lax.all_to_all(parts, axis, 0, 0, tiled=True)


def copies(rows, count):
    return jnp.broadcast_to(rows[None], (count, *rows.shape))


def pack(values):
    high = lax.reduce_precision(values, 8, 7)
    rest = values - high
    middle = lax.reduce_precision(rest, 8, 7)
    terms = jnp.stack([high, middle, rest - middle], axis=-2).astype(jnp.bfloat16)
    widths = [(0, 0)] * (terms.ndim - 2) + [(0, 5), (0, 128 - terms.shape[-1])]
    return jnp.pad(terms, widths)


def unpack(rows, width):
    terms = rows[..., :3, :width].astype(jnp.float32)
    return terms[..., 0, :] + (terms[..., 1, :] + terms[..., 2, :])


def sum_all(stacked):
    flat = stacked.reshape(-1, 128)
    partial = jnp.sum(swap(copies(flat, lax.axis_size(PLANE)), PLANE), axis=0)
    total = jnp.sum(swap(copies(partial, lax.axis_size(DEPTH)), DEPTH), axis=0)
    return total.reshape(stacked.shape)


def block_sums(selected, products, row_count):
    targets = jnp.arange(row_count, dtype=jnp.int32)
    picker = (targets[:, None] == selected[None, :]).astype(jnp.float32)
    return jnp.dot(picker, products, precision=highest)


def apply_operator(vectors, grams, tile_set, row_list, column_list, diagonal_blocks):
    narrow = vectors.astype(jnp.bfloat16)
    shape = narrow.shape
    own_blocks = shape[0]
    height = shape[0] * shape[1]
    own = narrow.reshape(height, shape[2])
    fars, columns = lax.axis_size(FAR), lax.axis_size(COLUMN)
    rows = 4 * fars
    count_tiles = tile_set.shape[0]
    width = grams.size // columns

    sent = jnp.concatenate(
        [copies(own, columns), pack(grams.reshape(columns, width))], axis=1
    )
    got = swap(sent, COLUMN)
    row_slab = got[:, :height].reshape(-1, *shape[1:])
    piece = jnp.sum(unpack(got[:, height:], width), axis=0)
    lower_part = jnp.einsum(
        "tki,tij->tkj", row_slab[row_list], tile_set, preferred_element_type=jnp.float32
    ).reshape(count_tiles, -1)
    lower = block_sums(column_list, lower_part, own_blocks * rows).astype(jnp.bfloat16)
    lower = lower.reshape(2, fars, 2, height, 128).transpose(0, 2, 1, 3, 4)
    sent = jnp.concatenate(
        [lower.reshape(4, fars * height, 128), copies(pack(piece), 4)], axis=1
    )
    got = swap(sent, NEAR)
    lower = jnp.sum(got[:, :-8].astype(jnp.float32), axis=0).astype(jnp.bfloat16)
    piece = jnp.sum(unpack(got[:, -8:], width), axis=0)
    sent = jnp.concatenate(
        [copies(own, fars), lower.reshape(fars, height, 128), copies(pack(piece), fars)], axis=1
    )
    got = swap(sent, FAR)
    from_columns = jnp.sum(got[:, height : 2 * height].astype(jnp.float32), axis=0)
    piece = jnp.sum(unpack(got[:, 2 * height :], width), axis=0)
    got = swap(copies(got[:, :height].reshape(fars * height, 128), 4), NEAR)
    column_slab = got.reshape(-1, *shape[1:])
    near_first = (column_list // (2 * own_blocks * fars)) * 2 + (column_list // own_blocks) % 2
    column_place = (
        near_first * fars + (column_list // (2 * own_blocks)) % fars
    ) * own_blocks + column_list % own_blocks
    upper_part = jnp.einsum(
        "tkj,tij->tki", column_slab[column_place], tile_set, preferred_element_type=jnp.float32
    ).reshape(count_tiles, -1)
    upper = block_sums(row_list, upper_part, own_blocks * columns).astype(jnp.bfloat16)
    sent = jnp.concatenate(
        [upper.reshape(columns, height, -1), copies(pack(piece), columns)], axis=1
    )
    got = swap(sent, COLUMN)
    from_rows = jnp.sum(got[:, :height].astype(jnp.float32), axis=0)
    diagonal = 0.5 * (
        jnp.einsum("bkj,bij->bki", narrow, diagonal_blocks, preferred_element_type=jnp.float32)
        + jnp.einsum("bki,bij->bkj", narrow, diagonal_blocks, preferred_element_type=jnp.float32)
    )
    image = (from_rows + from_columns).reshape(shape) + diagonal
    return image, unpack(got[:, height:], width).reshape(grams.shape)


def factor_of(gram):
    factor = jnp.linalg.cholesky(gram)
    inverse = jax.scipy.linalg.solve_triangular(
        factor, jnp.eye(factor.shape[0], dtype=jnp.float32), lower=True
    )
    return factor, inverse


def local(start_block, tile_values, tile_rows, tile_columns, diagonal_blocks):
    matrix = (tile_values[0, 0], tile_rows[0, 0], tile_columns[0, 0], diagonal_blocks)
    start_gram = gram_of(start_block, start_block)[None]
    first, start_sum = apply_operator(start_block, start_gram, *matrix)
    first_grams = jnp.stack([gram_of(start_block, first), gram_of(first, first)])
    second, sums = apply_operator(first, first_grams, *matrix)
    _, inverse_start = factor_of(start_sum[0])
    alpha_first = dot(dot(inverse_start, sums[0]), inverse_start.T)
    image_gram = dot(dot(inverse_start, sums[1]), inverse_start.T)
    beta_first, inverse_first = factor_of(image_gram - dot(alpha_first.T, alpha_first))
    basis_start = mix(inverse_start, start_block)
    image_start = mix(inverse_start, first)
    basis_first = mix(inverse_first, image_start - mix(alpha_first.T, basis_start))
    moved = mix(inverse_start, second) - mix(alpha_first.T, image_start)
    image_first = mix(inverse_first, moved) - mix(beta_first.T, basis_start)
    last = sum_all(jnp.stack([gram_of(basis_first, image_first), gram_of(image_first, image_first)]))
    alpha_last = last[0]
    beta_last, inverse_last = factor_of(last[1] - dot(alpha_last.T, alpha_last))
    basis_last = mix(inverse_last, image_first - mix(alpha_last.T, basis_first))
    scaling = math.sqrt(
        start_block.shape[0] * start_block.shape[2] * lax.axis_size(PLANE) * lax.axis_size(DEPTH)
    )
    return (
        basis_last * scaling,
        jnp.stack([alpha_first, alpha_last]),
        jnp.stack([beta_first, beta_last]),
    )


def solution(mesh):
    split = Mesh(mesh.devices.reshape(2, 8, 2, 2, 4, 2), AXES)
    rows = ("x_high", "far", "near")
    owner = P((*COLUMN, *rows), None, None)
    placed = (
        owner,
        P(rows, COLUMN, None, None, None),
        P(rows, COLUMN, None),
        P(rows, COLUMN, None),
        owner,
    )
    return jax.shard_map(
        local,
        mesh=split,
        in_specs=placed,
        out_specs=(owner, P(), P()),
        check_vma=False,
    )
```

```python
import functools
import math

import jax
import jax.numpy as jnp
from jax import lax
from jax.experimental import pallas as pl
from jax.experimental.pallas import tpu as pltpu
from jax.sharding import Mesh
from jax.sharding import PartitionSpec as P

AXES = ("x_high", "far", "near", "x_low", "y", "core")
COLUMN = ("x_low", "y", "core")
PLANE = ("x_high", *COLUMN)
DEPTH = ("far", "near")
NEAR = ("x_high", "near")
FAR = ("far",)

NEARS = 4
FARS = 8
COLUMNS = 16
K = 32
OWN = 64
SLAB = FARS * OWN
EXTRA = 16
TERMS = 3
GROUP = 8

highest = lax.Precision.HIGHEST
f32 = jnp.float32
bf16 = jnp.bfloat16


def swap(parts, axis):
    return lax.all_to_all(parts, axis, 0, 0, tiled=True)


def call(kernel, outs, scalars, arrays, scratch=()):
    specs = [pl.BlockSpec(memory_space=pltpu.SMEM)] * len(scalars)
    specs += [pl.BlockSpec(memory_space=pltpu.VMEM)] * len(arrays)
    return pl.pallas_call(
        kernel,
        out_shape=outs,
        in_specs=specs,
        out_specs=jax.tree.map(lambda _: pl.BlockSpec(memory_space=pltpu.VMEM), outs),
        scratch_shapes=list(scratch),
        compiler_params=pltpu.CompilerParams(vmem_limit_bytes=16 * 2**20),
    )(*scalars, *arrays)


def out(shape, dtype):
    return jax.ShapeDtypeStruct(shape, dtype)


def iota(shape, dimension):
    return lax.broadcasted_iota(jnp.int32, shape, dimension)


def dot(left, right):
    return jnp.dot(left, right, precision=highest, preferred_element_type=f32)


def dot_t(left, right, precision=highest):
    return lax.dot_general(
        left, right, (((1,), (1,)), ((), ())), precision=precision, preferred_element_type=f32
    )


def terms_of(values):
    high = values.astype(bf16)
    rest = values - high.astype(f32)
    middle = rest.astype(bf16)
    low = (rest - middle.astype(f32)).astype(bf16)
    return high, middle, low


def one_hot(condition):
    return jnp.where(condition, 1.0, 0.0).astype(bf16)


def spread_slices(grams):
    source = jnp.concatenate(terms_of(grams), axis=0)
    shape = (COLUMNS * EXTRA, TERMS * K)
    row, column = iota(shape, 0), iota(shape, 1)
    place = row & (EXTRA - 1)
    wanted = (place >> 1) * K + (row >> 4) * 2 + (place & 1)
    picker = one_hot((place < 2 * TERMS) & (column == wanted))
    return jnp.dot(picker, source, preferred_element_type=f32).astype(bf16)


def sum_slices(pieces):
    shape = (EXTRA, pieces.shape[0])
    row, column = iota(shape, 0), iota(shape, 1)
    picker = one_hot(((column & 15) < 2 * TERMS) & ((column & 1) == (row & 1)))
    total = jnp.dot(picker, pieces, preferred_element_type=f32)
    high, middle, low = (term.astype(f32) for term in terms_of(total))
    place = iota(total.shape, 0)
    chosen = jnp.where(place < 2, high, jnp.where(place < 4, middle, low))
    return jnp.where(place < 2 * TERMS, chosen, 0.0).astype(bf16)


def join_slices(pieces):
    shape = (K, pieces.shape[0])
    row, column = iota(shape, 0), iota(shape, 1)
    picker = one_hot(
        ((column >> 4) == (row >> 1)) & ((column & 15) < 2 * TERMS) & ((column & 1) == (row & 1))
    )
    return jnp.dot(picker, pieces, preferred_element_type=f32)


def factor_of(gram):
    shape = (K, 128)
    row, column = iota(shape, 0), iota(shape, 1)
    work = jnp.where(column < K, gram, jnp.where(column == row + K, 1.0, 0.0))
    for step in range(K):
        across = jnp.broadcast_to(work[:, step : step + 1], shape)
        pivot = across[step : step + 1, :]
        guess = lax.rsqrt(pivot)
        scale = guess * (1.5 - 0.5 * pivot * guess * guess)
        lead = work[step : step + 1, :] * scale
        lower = work - (across * scale) * lead
        work = jnp.where(row > step, lower, jnp.where(row == step, lead, work))
    upper = jnp.where((column < K) & (column >= row), work, 0.0)
    inverse = pltpu.roll(work, 128 - K, 1)
    return upper[:, :K], inverse[:, :K]


def flip(matrix):
    eye = jnp.where(iota((K, K), 0) == iota((K, K), 1), 1.0, 0.0)
    return dot_t(eye, matrix)


def shifted(block, place, places):
    empty = jnp.zeros_like(block)
    return jnp.concatenate([block if i == place else empty for i in range(places)], axis=0)


def fill_first(message, narrow, grams):
    message[:, OWN:, :] = spread_slices(grams).reshape(COLUMNS, EXTRA, 128)
    for device in range(COLUMNS):
        message[device, :OWN, :] = narrow


def prepare_kernel(start, message):
    grams = jnp.zeros((K, 128), f32)
    for block in range(OWN // K):
        vectors = start[block * K : (block + 1) * K, :]
        grams += dot_t(vectors, shifted(vectors, 0, 4))
    fill_first(message, start[...].astype(bf16), grams)


def lower_kernel(rows, columns, got, tiles, message, total):
    total[...] = jnp.zeros_like(total)
    count = tiles.shape[0]
    for base in range(0, count, GROUP):
        parts = []
        for tile in range(base, base + GROUP):
            place = rows[tile]
            vectors = got[place >> 1, pl.ds(pl.multiple_of((place & 1) * K, K), K), :]
            parts.append(jnp.dot(vectors, tiles[tile], preferred_element_type=f32))
        for tile in range(base, base + GROUP):
            place = columns[tile]
            owner = place >> 1
            near = (owner >> 4) * 2 + (owner & 1)
            spot = (near * FARS + ((owner >> 1) & 7)) * 2 + (place & 1)
            where = pl.ds(pl.multiple_of(spot * K, K), K)
            total[where, :] += parts[tile - base]
    message[:, :SLAB, :] = total[...].astype(bf16).reshape(NEARS, SLAB, 128)
    piece = sum_slices(got[:, OWN:, :].reshape(COLUMNS * EXTRA, 128))
    for device in range(NEARS):
        message[device, SLAB:, :] = piece


def near_kernel(got, vectors, message):
    total = got[0, :SLAB, :].astype(f32)
    for device in range(1, NEARS):
        total += got[device, :SLAB, :].astype(f32)
    message[:, OWN : 2 * OWN, :] = total.astype(bf16).reshape(FARS, OWN, 128)
    piece = sum_slices(got[:, SLAB:, :].reshape(NEARS * EXTRA, 128))
    narrow = vectors[...].astype(bf16)
    for device in range(FARS):
        message[device, :OWN, :] = narrow
        message[device, 2 * OWN :, :] = piece


def far_kernel(got, message, column_sums, piece):
    total = got[0, OWN : 2 * OWN, :].astype(f32)
    for device in range(1, FARS):
        total += got[device, OWN : 2 * OWN, :].astype(f32)
    column_sums[...] = total
    piece[...] = sum_slices(got[:, 2 * OWN :, :].reshape(FARS * EXTRA, 128))
    slab = got[:, :OWN, :].reshape(SLAB, 128)
    for device in range(NEARS):
        message[device, :, :] = slab


def upper_kernel(rows, columns, got, tiles, piece, message, total):
    total[...] = jnp.zeros_like(total)
    count = tiles.shape[0]
    for base in range(0, count, GROUP):
        parts = []
        for tile in range(base, base + GROUP):
            place = columns[tile]
            owner = place >> 1
            near = (owner >> 4) * 2 + (owner & 1)
            spot = ((owner >> 1) & 7) * 2 + (place & 1)
            vectors = got[near, pl.ds(pl.multiple_of(spot * K, K), K), :]
            parts.append(dot_t(vectors, tiles[tile], None))
        for tile in range(base, base + GROUP):
            where = pl.ds(pl.multiple_of(rows[tile] * K, K), K)
            total[where, :] += parts[tile - base]
    message[:, :OWN, :] = total[...].astype(bf16).reshape(COLUMNS, OWN, 128)
    for device in range(COLUMNS):
        message[device, OWN:, :] = piece[...]


def image_of(got, column_sums, vectors, diagonal):
    images = []
    for block in range(OWN // K):
        where = slice(block * K, (block + 1) * K)
        narrow = vectors[where, :].astype(bf16)
        image = dot_t(narrow, diagonal[block], None)
        image += jnp.dot(narrow, diagonal[block], preferred_element_type=f32)
        image = 0.5 * image + column_sums[where, :]
        total = got[0, where, :].astype(f32)
        for device in range(1, COLUMNS):
            total += got[device, where, :].astype(f32)
        images.append(image + total)
    return images


def middle_kernel(got, column_sums, start, diagonal, image, start_sum, message):
    images = image_of(got, column_sums, start, diagonal)
    start_sum[...] = join_slices(got[:, OWN:, :].reshape(COLUMNS * EXTRA, 128))
    grams = jnp.zeros((K, 128), f32)
    for block in range(OWN // K):
        where = slice(block * K, (block + 1) * K)
        image[where, :] = images[block]
        joint = jnp.concatenate([start[where, :], images[block]] + [jnp.zeros((K, 128), f32)] * 2)
        grams += dot_t(images[block], joint)
    fill_first(message, jnp.concatenate(images).astype(bf16), grams)


def factor_kernel(gram, inverse):
    inverse[...] = factor_of(gram[...])[1]


def finish_kernel(
    got, column_sums, start, first, diagonal, inverse_start, basis, image, alpha, beta, message
):
    images = image_of(got, column_sums, first, diagonal)
    sums = join_slices(got[:, OWN:, :].reshape(COLUMNS * EXTRA, 128))
    inverse = inverse_start[...]
    alpha_t = dot_t(dot(inverse, sums[:, :K]), inverse)
    image_gram = dot_t(dot(inverse, pltpu.roll(sums, 128 - K, 1)[:, :K]), inverse)
    wide = jnp.zeros((128 - K, K), f32)
    square = dot_t(alpha_t, jnp.concatenate([alpha_t, wide]))
    upper, inverse_first = factor_of(
        jnp.concatenate([image_gram, jnp.zeros((K, 128 - K), f32)], axis=1) - square
    )
    packed = jnp.zeros((K // 2, 128), f32)
    for block in range(OWN // K):
        where = slice(block * K, (block + 1) * K)
        basis_start = dot(inverse, start[where, :])
        image_start = dot(inverse, first[where, :])
        current = dot(inverse_first, image_start - dot(alpha_t, basis_start))
        moved = dot(inverse, images[block]) - dot(alpha_t, image_start)
        result = dot(inverse_first, moved) - dot(upper, basis_start)
        basis[where, :] = current
        image[where, :] = result
        for half in range(2):
            top = result[half * (K // 2) : (half + 1) * (K // 2), :]
            empty = jnp.zeros_like(result)
            pair = [current, empty, result, empty] if half == 0 else [empty, current, empty, result]
            packed += dot_t(top, jnp.concatenate(pair))
    for device in range(message.shape[0]):
        message[device, :, :] = packed
    alpha[...] = flip(alpha_t)
    beta[...] = flip(upper)


def plane_kernel(got, message):
    total = got[0]
    for device in range(1, got.shape[0]):
        total += got[device]
    for device in range(message.shape[0]):
        message[device, :, :] = total


def last_kernel(scaling, got, basis, image, result, alpha, beta):
    total = got[0]
    for device in range(1, got.shape[0]):
        total += got[device]
    turned = [total] + [pltpu.roll(total, 128 - K * place, 1) for place in range(1, 4)]
    alpha_t = jnp.concatenate(turned[:2])[:, :K]
    image_gram = jnp.concatenate(turned[2:])
    wide = jnp.zeros((128 - K, K), f32)
    square = dot_t(alpha_t, jnp.concatenate([alpha_t, wide]))
    upper, inverse = factor_of(image_gram - square)
    for block in range(OWN // K):
        where = slice(block * K, (block + 1) * K)
        residual = image[where, :] - dot(alpha_t, basis[where, :])
        result[where, :] = dot(inverse, residual) * scaling
    alpha[...] = flip(alpha_t)
    beta[...] = flip(upper)


def exchange(message, vectors, tiles, rows, columns):
    got = swap(message, COLUMN)
    sent = call(
        lower_kernel,
        out((NEARS, SLAB + EXTRA, 128), bf16),
        (rows, columns),
        (got, tiles),
        (pltpu.VMEM((NEARS * SLAB, 128), f32),),
    )
    got = swap(sent, NEAR)
    sent = call(near_kernel, out((FARS, 2 * OWN + EXTRA, 128), bf16), (), (got, vectors))
    got = swap(sent, FAR)
    sent, column_sums, piece = call(
        far_kernel,
        (out((NEARS, SLAB, 128), bf16), out((OWN, 128), f32), out((EXTRA, 128), bf16)),
        (),
        (got,),
    )
    got = swap(sent, NEAR)
    sent = call(
        upper_kernel,
        out((COLUMNS, OWN + EXTRA, 128), bf16),
        (rows, columns),
        (got, tiles, piece),
        (pltpu.VMEM((COLUMNS * OWN, 128), f32),),
    )
    return swap(sent, COLUMN), column_sums


def local(start_block, tile_values, tile_rows, tile_columns, diagonal_blocks):
    start = start_block.reshape(OWN, 128)
    matrix = (tile_values[0, 0], tile_rows[0, 0], tile_columns[0, 0])
    first_message = out((COLUMNS, OWN + EXTRA, 128), bf16)
    vectors = out((OWN, 128), f32)
    square = out((K, K), f32)
    message = call(prepare_kernel, first_message, (), (start,))
    got, column_sums = exchange(message, start, *matrix)
    first, start_sum, message = call(
        middle_kernel,
        (vectors, out((K, 128), f32), first_message),
        (),
        (got, column_sums, start, diagonal_blocks),
    )
    inverse_start = call(factor_kernel, square, (), (start_sum,))
    got, column_sums = exchange(message, first, *matrix)
    planes, depths = lax.axis_size(PLANE), lax.axis_size(DEPTH)
    basis, image, alpha_first, beta_first, message = call(
        finish_kernel,
        (vectors, vectors, square, square, out((planes, K // 2, 128), f32)),
        (),
        (got, column_sums, start, first, diagonal_blocks, inverse_start),
    )
    got = swap(message, PLANE)
    message = call(plane_kernel, out((depths, K // 2, 128), f32), (), (got,))
    got = swap(message, DEPTH)
    scaling = math.sqrt(start_block.shape[0] * start_block.shape[2] * planes * depths)
    result, alpha_last, beta_last = call(
        functools.partial(last_kernel, scaling),
        (vectors, square, square),
        (),
        (got, basis, image),
    )
    return (
        result.reshape(start_block.shape),
        jnp.stack([alpha_first, alpha_last]),
        jnp.stack([beta_first, beta_last]),
    )


def solution(mesh):
    split = Mesh(mesh.devices.reshape(2, FARS, 2, 2, 4, 2), AXES)
    rows = ("x_high", "far", "near")
    owner = P((*COLUMN, *rows), None, None)
    placed = (
        owner,
        P(rows, COLUMN, None, None, None),
        P(rows, COLUMN, None),
        P(rows, COLUMN, None),
        owner,
    )
    return jax.shard_map(
        local,
        mesh=split,
        in_specs=placed,
        out_specs=(owner, P(), P()),
        check_vma=False,
    )
```

```python
import functools
import math

import jax
import jax.numpy as jnp
from jax import lax
from jax.experimental import pallas as pl
from jax.experimental.pallas import tpu as pltpu
from jax.sharding import Mesh
from jax.sharding import PartitionSpec as P

AXES = ("x_high", "far", "near", "x_low", "y", "core")
COLUMN = ("x_low", "y", "core")
PLANE = ("x_high", *COLUMN)
DEPTH = ("far", "near")
NEAR = ("x_high", "near")
FAR = ("far",)

NEARS = 4
FARS = 8
COLUMNS = 16
K = 32
OWN = 64
SLAB = FARS * OWN
EXTRA = 16
TERMS = 3
GROUP = 8
PANEL = 8

highest = lax.Precision.HIGHEST
f32 = jnp.float32
bf16 = jnp.bfloat16


def swap(parts, axis):
    return lax.all_to_all(parts, axis, 0, 0, tiled=True)


def call(kernel, outs, scalars, arrays, scratch=()):
    specs = [pl.BlockSpec(memory_space=pltpu.SMEM)] * len(scalars)
    specs += [pl.BlockSpec(memory_space=pltpu.VMEM)] * len(arrays)
    return pl.pallas_call(
        kernel,
        out_shape=outs,
        in_specs=specs,
        out_specs=jax.tree.map(lambda _: pl.BlockSpec(memory_space=pltpu.VMEM), outs),
        scratch_shapes=list(scratch),
        compiler_params=pltpu.CompilerParams(vmem_limit_bytes=16 * 2**20),
    )(*scalars, *arrays)


def out(shape, dtype):
    return jax.ShapeDtypeStruct(shape, dtype)


def iota(shape, dimension):
    return lax.broadcasted_iota(jnp.int32, shape, dimension)


def dot(left, right):
    return jnp.dot(left, right, precision=highest, preferred_element_type=f32)


def dot_t(left, right, precision=highest):
    return lax.dot_general(
        left, right, (((1,), (1,)), ((), ())), precision=precision, preferred_element_type=f32
    )


def terms_of(values):
    high = values.astype(bf16)
    rest = values - high.astype(f32)
    middle = rest.astype(bf16)
    low = (rest - middle.astype(f32)).astype(bf16)
    return high, middle, low


def one_hot(condition):
    return jnp.where(condition, 1.0, 0.0).astype(bf16)


def spread_slices(grams):
    source = jnp.concatenate(terms_of(grams), axis=0)
    shape = (COLUMNS * EXTRA, TERMS * K)
    row, column = iota(shape, 0), iota(shape, 1)
    place = row & (EXTRA - 1)
    wanted = (place >> 1) * K + (row >> 4) * 2 + (place & 1)
    picker = one_hot((place < 2 * TERMS) & (column == wanted))
    return jnp.dot(picker, source, preferred_element_type=f32).astype(bf16)


def sum_slices(pieces):
    shape = (EXTRA, pieces.shape[0])
    row, column = iota(shape, 0), iota(shape, 1)
    picker = one_hot(((column & 15) < 2 * TERMS) & ((column & 1) == (row & 1)))
    total = jnp.dot(picker, pieces, preferred_element_type=f32)
    high, middle, low = (term.astype(f32) for term in terms_of(total))
    place = iota(total.shape, 0)
    chosen = jnp.where(place < 2, high, jnp.where(place < 4, middle, low))
    return jnp.where(place < 2 * TERMS, chosen, 0.0).astype(bf16)


def join_slices(pieces):
    shape = (K, pieces.shape[0])
    row, column = iota(shape, 0), iota(shape, 1)
    picker = one_hot(
        ((column >> 4) == (row >> 1)) & ((column & 15) < 2 * TERMS) & ((column & 1) == (row & 1))
    )
    return jnp.dot(picker, pieces, preferred_element_type=f32)


def factor_of(gram):
    shape = (K, 128)
    row, column = iota(shape, 0), iota(shape, 1)
    work = jnp.where(column < K, gram, jnp.where(column == row + K, 1.0, 0.0))
    for base in range(0, K, PANEL):
        columns = [
            jnp.broadcast_to(work[:, base + step : base + step + 1], shape) for step in range(PANEL)
        ]
        leads = [work[base + step : base + step + 1, :] for step in range(PANEL)]
        for step in range(PANEL):
            scale = lax.rsqrt(columns[step][base + step : base + step + 1, :])
            columns[step] *= scale
            leads[step] *= scale
            for later in range(step + 1, PANEL):
                share = columns[step][base + later : base + later + 1, :]
                columns[later] -= columns[step] * share
                leads[later] -= leads[step] * share
        lower = work
        for step in range(PANEL):
            lower -= columns[step] * leads[step]
        work = jnp.where(row >= base + PANEL, lower, work)
        for step in range(PANEL):
            work = jnp.where(row == base + step, leads[step], work)
    upper = jnp.where((column < K) & (column >= row), work, 0.0)
    inverse = pltpu.roll(work, 128 - K, 1)
    return upper[:, :K], inverse[:, :K]


def flip(matrix):
    eye = jnp.where(iota((K, K), 0) == iota((K, K), 1), 1.0, 0.0)
    return dot_t(eye, matrix)


def shifted(block, place, places):
    empty = jnp.zeros_like(block)
    return jnp.concatenate([block if i == place else empty for i in range(places)], axis=0)


def fill_first(message, narrow, grams):
    message[:, OWN:, :] = spread_slices(grams).reshape(COLUMNS, EXTRA, 128)
    for device in range(COLUMNS):
        message[device, :OWN, :] = narrow


def stage_kernel(tiles, staged):
    staged[...] = tiles[...]


def prepare_kernel(start, message):
    grams = jnp.zeros((K, 128), f32)
    for block in range(OWN // K):
        vectors = start[block * K : (block + 1) * K, :]
        grams += dot_t(vectors, shifted(vectors, 0, 4))
    fill_first(message, start[...].astype(bf16), grams)


def lower_kernel(lists, got, tiles, message, total):
    total[...] = jnp.zeros_like(total)
    count = tiles.shape[0]
    for base in range(0, count, GROUP):
        parts = []
        for tile in range(base, base + GROUP):
            place = lists[tile]
            vectors = got[place >> 1, pl.ds(pl.multiple_of((place & 1) * K, K), K), :]
            parts.append(jnp.dot(vectors, tiles[tile], preferred_element_type=f32))
        for tile in range(base, base + GROUP):
            place = lists[count + tile]
            owner = place >> 1
            near = (owner >> 4) * 2 + (owner & 1)
            spot = (near * FARS + ((owner >> 1) & 7)) * 2 + (place & 1)
            where = pl.ds(pl.multiple_of(spot * K, K), K)
            total[where, :] += parts[tile - base]
    message[:, :SLAB, :] = total[...].astype(bf16).reshape(NEARS, SLAB, 128)
    piece = sum_slices(got[:, OWN:, :].reshape(COLUMNS * EXTRA, 128))
    for device in range(NEARS):
        message[device, SLAB:, :] = piece


def near_kernel(got, vectors, message):
    total = got[0, :SLAB, :].astype(f32)
    for device in range(1, NEARS):
        total += got[device, :SLAB, :].astype(f32)
    message[:, OWN : 2 * OWN, :] = total.astype(bf16).reshape(FARS, OWN, 128)
    piece = sum_slices(got[:, SLAB:, :].reshape(NEARS * EXTRA, 128))
    narrow = vectors[...].astype(bf16)
    for device in range(FARS):
        message[device, :OWN, :] = narrow
        message[device, 2 * OWN :, :] = piece


def far_kernel(got, message, column_sums, piece):
    total = got[0, OWN : 2 * OWN, :].astype(f32)
    for device in range(1, FARS):
        total += got[device, OWN : 2 * OWN, :].astype(f32)
    column_sums[...] = total
    piece[...] = sum_slices(got[:, 2 * OWN :, :].reshape(FARS * EXTRA, 128))
    slab = got[:, :OWN, :].reshape(SLAB, 128)
    for device in range(NEARS):
        message[device, :, :] = slab


def upper_kernel(lists, got, tiles, piece, message, total):
    total[...] = jnp.zeros_like(total)
    count = tiles.shape[0]
    for base in range(0, count, GROUP):
        parts = []
        for tile in range(base, base + GROUP):
            place = lists[count + tile]
            owner = place >> 1
            near = (owner >> 4) * 2 + (owner & 1)
            spot = ((owner >> 1) & 7) * 2 + (place & 1)
            vectors = got[near, pl.ds(pl.multiple_of(spot * K, K), K), :]
            parts.append(dot_t(vectors, tiles[tile], None))
        for tile in range(base, base + GROUP):
            where = pl.ds(pl.multiple_of(lists[tile] * K, K), K)
            total[where, :] += parts[tile - base]
    message[:, :OWN, :] = total[...].astype(bf16).reshape(COLUMNS, OWN, 128)
    for device in range(COLUMNS):
        message[device, OWN:, :] = piece[...]


def image_of(got, column_sums, vectors, diagonal):
    images = []
    for block in range(OWN // K):
        where = slice(block * K, (block + 1) * K)
        narrow = vectors[where, :].astype(bf16)
        image = dot_t(narrow, diagonal[block], None)
        image += jnp.dot(narrow, diagonal[block], preferred_element_type=f32)
        image = 0.5 * image + column_sums[where, :]
        total = got[0, where, :].astype(f32)
        for device in range(1, COLUMNS):
            total += got[device, where, :].astype(f32)
        images.append(image + total)
    return images


def middle_kernel(got, column_sums, start, diagonal, image, start_sum, message):
    images = image_of(got, column_sums, start, diagonal)
    start_sum[...] = join_slices(got[:, OWN:, :].reshape(COLUMNS * EXTRA, 128))
    grams = jnp.zeros((K, 128), f32)
    for block in range(OWN // K):
        where = slice(block * K, (block + 1) * K)
        image[where, :] = images[block]
        joint = jnp.concatenate([start[where, :], images[block]] + [jnp.zeros((K, 128), f32)] * 2)
        grams += dot_t(images[block], joint)
    fill_first(message, jnp.concatenate(images).astype(bf16), grams)


def factor_kernel(gram, inverse):
    inverse[...] = factor_of(gram[...])[1]


def finish_kernel(
    got, column_sums, start, first, diagonal, inverse_start, basis, image, alpha, beta, message
):
    images = image_of(got, column_sums, first, diagonal)
    sums = join_slices(got[:, OWN:, :].reshape(COLUMNS * EXTRA, 128))
    inverse = inverse_start[...]
    alpha_t = dot_t(dot(inverse, sums[:, :K]), inverse)
    image_gram = dot_t(dot(inverse, pltpu.roll(sums, 128 - K, 1)[:, :K]), inverse)
    wide = jnp.zeros((128 - K, K), f32)
    square = dot_t(alpha_t, jnp.concatenate([alpha_t, wide]))
    upper, inverse_first = factor_of(
        jnp.concatenate([image_gram, jnp.zeros((K, 128 - K), f32)], axis=1) - square
    )
    packed = jnp.zeros((K // 2, 128), f32)
    for block in range(OWN // K):
        where = slice(block * K, (block + 1) * K)
        basis_start = dot(inverse, start[where, :])
        image_start = dot(inverse, first[where, :])
        current = dot(inverse_first, image_start - dot(alpha_t, basis_start))
        moved = dot(inverse, images[block]) - dot(alpha_t, image_start)
        result = dot(inverse_first, moved) - dot(upper, basis_start)
        basis[where, :] = current
        image[where, :] = result
        for half in range(2):
            top = result[half * (K // 2) : (half + 1) * (K // 2), :]
            empty = jnp.zeros_like(result)
            pair = [current, empty, result, empty] if half == 0 else [empty, current, empty, result]
            packed += dot_t(top, jnp.concatenate(pair))
    for device in range(message.shape[0]):
        message[device, :, :] = packed
    alpha[...] = flip(alpha_t)
    beta[...] = flip(upper)


def plane_kernel(got, message):
    total = got[0]
    for device in range(1, got.shape[0]):
        total += got[device]
    for device in range(message.shape[0]):
        message[device, :, :] = total


def last_kernel(scaling, got, basis, image, alpha_first, beta_first, result, alphas, betas):
    total = got[0]
    for device in range(1, got.shape[0]):
        total += got[device]
    turned = [total] + [pltpu.roll(total, 128 - K * place, 1) for place in range(1, 4)]
    alpha_t = jnp.concatenate(turned[:2])[:, :K]
    image_gram = jnp.concatenate(turned[2:])
    wide = jnp.zeros((128 - K, K), f32)
    square = dot_t(alpha_t, jnp.concatenate([alpha_t, wide]))
    upper, inverse = factor_of(image_gram - square)
    for block in range(OWN // K):
        where = slice(block * K, (block + 1) * K)
        residual = image[where, :] - dot(alpha_t, basis[where, :])
        result[where, :] = dot(inverse, residual) * scaling
    alphas[0] = alpha_first[...]
    alphas[1] = flip(alpha_t)
    betas[0] = beta_first[...]
    betas[1] = flip(upper)


def exchange(message, vectors, tiles, lists):
    got = swap(message, COLUMN)
    sent = call(
        lower_kernel,
        out((NEARS, SLAB + EXTRA, 128), bf16),
        (lists,),
        (got, tiles),
        (pltpu.VMEM((NEARS * SLAB, 128), f32),),
    )
    got = swap(sent, NEAR)
    sent = call(near_kernel, out((FARS, 2 * OWN + EXTRA, 128), bf16), (), (got, vectors))
    got = swap(sent, FAR)
    sent, column_sums, piece = call(
        far_kernel,
        (out((NEARS, SLAB, 128), bf16), out((OWN, 128), f32), out((EXTRA, 128), bf16)),
        (),
        (got,),
    )
    got = swap(sent, NEAR)
    sent = call(
        upper_kernel,
        out((COLUMNS, OWN + EXTRA, 128), bf16),
        (lists,),
        (got, tiles, piece),
        (pltpu.VMEM((COLUMNS * OWN, 128), f32),),
    )
    return swap(sent, COLUMN), column_sums


def local(start_block, tile_values, tile_rows, tile_columns, diagonal_blocks):
    start = start_block.reshape(OWN, 128)
    tiles = tile_values[0, 0]
    matrix = (
        call(stage_kernel, out(tiles.shape, bf16), (), (tiles,)),
        jnp.concatenate([tile_rows[0, 0], tile_columns[0, 0]]),
    )
    first_message = out((COLUMNS, OWN + EXTRA, 128), bf16)
    vectors = out((OWN, 128), f32)
    square = out((K, K), f32)
    message = call(prepare_kernel, first_message, (), (start,))
    got, column_sums = exchange(message, start, *matrix)
    first, start_sum, message = call(
        middle_kernel,
        (vectors, out((K, 128), f32), first_message),
        (),
        (got, column_sums, start, diagonal_blocks),
    )
    inverse_start = call(factor_kernel, square, (), (start_sum,))
    got, column_sums = exchange(message, first, *matrix)
    planes, depths = lax.axis_size(PLANE), lax.axis_size(DEPTH)
    basis, image, alpha_first, beta_first, message = call(
        finish_kernel,
        (vectors, vectors, square, square, out((planes, K // 2, 128), f32)),
        (),
        (got, column_sums, start, first, diagonal_blocks, inverse_start),
    )
    got = swap(message, PLANE)
    message = call(plane_kernel, out((depths, K // 2, 128), f32), (), (got,))
    got = swap(message, DEPTH)
    scaling = math.sqrt(start_block.shape[0] * start_block.shape[2] * planes * depths)
    pair = out((2, K, K), f32)
    result, alphas, betas = call(
        functools.partial(last_kernel, scaling),
        (vectors, pair, pair),
        (),
        (got, basis, image, alpha_first, beta_first),
    )
    return result.reshape(start_block.shape), alphas, betas


def solution(mesh):
    split = Mesh(mesh.devices.reshape(2, FARS, 2, 2, 4, 2), AXES)
    rows = ("x_high", "far", "near")
    owner = P((*COLUMN, *rows), None, None)
    placed = (
        owner,
        P(rows, COLUMN, None, None, None),
        P(rows, COLUMN, None),
        P(rows, COLUMN, None),
        owner,
    )
    return jax.shard_map(
        local,
        mesh=split,
        in_specs=placed,
        out_specs=(owner, P(), P()),
        check_vma=False,
    )
```

```python
import functools
import math

import jax
import jax.numpy as jnp
from jax import lax
from jax.experimental import pallas as pl
from jax.experimental.pallas import tpu as pltpu
from jax.sharding import Mesh
from jax.sharding import PartitionSpec as P

AXES = ("x_high", "far", "near", "x_low", "y", "core")
COLUMN = ("x_low", "y", "core")
PLANE = ("x_high", *COLUMN)
DEPTH = ("far", "near")
NEAR = ("x_high", "near")
FAR = ("far",)

NEARS = 4
FARS = 8
COLUMNS = 16
K = 32
OWN = 64
SLAB = FARS * OWN
EXTRA = 16
TERMS = 3
GROUP = 8
PANEL = 8

highest = lax.Precision.HIGHEST
f32 = jnp.float32
bf16 = jnp.bfloat16


def swap(parts, axis):
    return lax.all_to_all(parts, axis, 0, 0, tiled=True)


def call(kernel, outs, scalars, arrays, scratch=()):
    specs = [pl.BlockSpec(memory_space=pltpu.SMEM)] * len(scalars)
    specs += [pl.BlockSpec(memory_space=pltpu.VMEM)] * len(arrays)
    return pl.pallas_call(
        kernel,
        out_shape=outs,
        in_specs=specs,
        out_specs=jax.tree.map(lambda _: pl.BlockSpec(memory_space=pltpu.VMEM), outs),
        scratch_shapes=list(scratch),
        compiler_params=pltpu.CompilerParams(vmem_limit_bytes=16 * 2**20),
    )(*scalars, *arrays)


def out(shape, dtype):
    return jax.ShapeDtypeStruct(shape, dtype)


def iota(shape, dimension):
    return lax.broadcasted_iota(jnp.int32, shape, dimension)


def dot(left, right):
    return jnp.dot(left, right, precision=highest, preferred_element_type=f32)


def dot_t(left, right, precision=highest):
    return lax.dot_general(
        left, right, (((1,), (1,)), ((), ())), precision=precision, preferred_element_type=f32
    )


def terms_of(values):
    high = values.astype(bf16)
    rest = values - high.astype(f32)
    middle = rest.astype(bf16)
    low = (rest - middle.astype(f32)).astype(bf16)
    return high, middle, low


def one_hot(condition):
    return jnp.where(condition, 1.0, 0.0).astype(bf16)


def spread_slices(grams):
    source = jnp.concatenate(terms_of(grams), axis=0)
    shape = (COLUMNS * EXTRA, TERMS * K)
    row, column = iota(shape, 0), iota(shape, 1)
    place = row & (EXTRA - 1)
    wanted = (place >> 1) * K + (row >> 4) * 2 + (place & 1)
    picker = one_hot((place < 2 * TERMS) & (column == wanted))
    return jnp.dot(picker, source, preferred_element_type=f32).astype(bf16)


def sum_slices(pieces):
    shape = (EXTRA, pieces.shape[0])
    row, column = iota(shape, 0), iota(shape, 1)
    picker = one_hot(((column & 15) < 2 * TERMS) & ((column & 1) == (row & 1)))
    total = jnp.dot(picker, pieces, preferred_element_type=f32)
    high, middle, low = (term.astype(f32) for term in terms_of(total))
    place = iota(total.shape, 0)
    chosen = jnp.where(place < 2, high, jnp.where(place < 4, middle, low))
    return jnp.where(place < 2 * TERMS, chosen, 0.0).astype(bf16)


def join_slices(pieces):
    shape = (K, pieces.shape[0])
    row, column = iota(shape, 0), iota(shape, 1)
    picker = one_hot(
        ((column >> 4) == (row >> 1)) & ((column & 15) < 2 * TERMS) & ((column & 1) == (row & 1))
    )
    return jnp.dot(picker, pieces, preferred_element_type=f32)


def factor_of(gram):
    shape = (K, 128)
    row, column = iota(shape, 0), iota(shape, 1)
    work = jnp.where(column < K, gram, jnp.where(column == row + K, 1.0, 0.0))
    for base in range(0, K, PANEL):
        columns = [
            jnp.broadcast_to(work[:, base + step : base + step + 1], shape) for step in range(PANEL)
        ]
        leads = [work[base + step : base + step + 1, :] for step in range(PANEL)]
        for step in range(PANEL):
            scale = lax.rsqrt(columns[step][base + step : base + step + 1, :])
            columns[step] *= scale
            leads[step] *= scale
            for later in range(step + 1, PANEL):
                share = columns[step][base + later : base + later + 1, :]
                columns[later] -= columns[step] * share
                leads[later] -= leads[step] * share
        lower = work
        for step in range(PANEL):
            lower -= columns[step] * leads[step]
        work = jnp.where(row >= base + PANEL, lower, work)
        for step in range(PANEL):
            work = jnp.where(row == base + step, leads[step], work)
    upper = jnp.where((column < K) & (column >= row), work, 0.0)
    inverse = pltpu.roll(work, 128 - K, 1)
    return upper[:, :K], inverse[:, :K]


def flip(matrix):
    eye = jnp.where(iota((K, K), 0) == iota((K, K), 1), 1.0, 0.0)
    return dot_t(eye, matrix)


def fill(message, rows):
    for device in range(message.shape[0]):
        message[device, : rows.shape[0], :] = rows


def stage_kernel(tiles, staged):
    staged[...] = tiles[...]


def prepare_kernel(start, message):
    fill(message, start[...].astype(bf16))


def lower_kernel(lists, got, tiles, message, total):
    total[...] = jnp.zeros_like(total)
    count = tiles.shape[0]
    for base in range(0, count, GROUP):
        parts = []
        for tile in range(base, base + GROUP):
            place = lists[tile]
            vectors = got[place >> 1, pl.ds(pl.multiple_of((place & 1) * K, K), K), :]
            parts.append(jnp.dot(vectors, tiles[tile], preferred_element_type=f32))
        for tile in range(base, base + GROUP):
            place = lists[count + tile]
            owner = place >> 1
            near = (owner >> 4) * 2 + (owner & 1)
            spot = (near * FARS + ((owner >> 1) & 7)) * 2 + (place & 1)
            where = pl.ds(pl.multiple_of(spot * K, K), K)
            total[where, :] += parts[tile - base]
    message[:, :SLAB, :] = total[...].astype(bf16).reshape(NEARS, SLAB, 128)
    if got.shape[1] > OWN:
        piece = sum_slices(got[:, OWN:, :].reshape(COLUMNS * EXTRA, 128))
        for device in range(NEARS):
            message[device, SLAB:, :] = piece


def near_kernel(got, vectors, message):
    total = got[0, :SLAB, :].astype(f32)
    for device in range(1, NEARS):
        total += got[device, :SLAB, :].astype(f32)
    message[:, OWN : 2 * OWN, :] = total.astype(bf16).reshape(FARS, OWN, 128)
    fill(message, vectors[...].astype(bf16))
    if got.shape[1] > SLAB:
        piece = sum_slices(got[:, SLAB:, :].reshape(NEARS * EXTRA, 128))
        for device in range(FARS):
            message[device, 2 * OWN :, :] = piece


def far_kernel(got, message, column_sums, *piece):
    total = got[0, OWN : 2 * OWN, :].astype(f32)
    for device in range(1, FARS):
        total += got[device, OWN : 2 * OWN, :].astype(f32)
    column_sums[...] = total
    if piece:
        piece[0][...] = sum_slices(got[:, 2 * OWN :, :].reshape(FARS * EXTRA, 128))
    fill(message, got[:, :OWN, :].reshape(SLAB, 128))


def upper_kernel(lists, got, tiles, *refs):
    *piece, message, total = refs
    total[...] = jnp.zeros_like(total)
    count = tiles.shape[0]
    for base in range(0, count, GROUP):
        parts = []
        for tile in range(base, base + GROUP):
            place = lists[count + tile]
            owner = place >> 1
            near = (owner >> 4) * 2 + (owner & 1)
            spot = ((owner >> 1) & 7) * 2 + (place & 1)
            vectors = got[near, pl.ds(pl.multiple_of(spot * K, K), K), :]
            parts.append(dot_t(vectors, tiles[tile], None))
        for tile in range(base, base + GROUP):
            where = pl.ds(pl.multiple_of(lists[tile] * K, K), K)
            total[where, :] += parts[tile - base]
    message[:, :OWN, :] = total[...].astype(bf16).reshape(COLUMNS, OWN, 128)
    if piece:
        for device in range(COLUMNS):
            message[device, OWN:, :] = piece[0][...]


def image_of(got, column_sums, vectors, diagonal):
    images = []
    for block in range(OWN // K):
        where = slice(block * K, (block + 1) * K)
        narrow = vectors[where, :].astype(bf16)
        image = dot_t(narrow, diagonal[block], None)
        image += jnp.dot(narrow, diagonal[block], preferred_element_type=f32)
        image = 0.5 * image + column_sums[where, :]
        total = got[0, where, :].astype(f32)
        for device in range(1, COLUMNS):
            total += got[device, where, :].astype(f32)
        images.append(image + total)
    return images


def middle_kernel(got, column_sums, start, diagonal, image, message):
    images = image_of(got, column_sums, start, diagonal)
    grams = jnp.zeros((K, 128), f32)
    empty = jnp.zeros((K, 128), f32)
    for block in range(OWN // K):
        where = slice(block * K, (block + 1) * K)
        vectors = start[where, :]
        image[where, :] = images[block]
        grams += dot_t(vectors, jnp.concatenate([vectors, empty, empty, empty]))
        grams += dot_t(images[block], jnp.concatenate([empty, vectors, images[block], empty]))
    fill(message, jnp.concatenate(images).astype(bf16))
    message[:, OWN:, :] = spread_slices(grams).reshape(COLUMNS, EXTRA, 128)


def finish_kernel(
    got, column_sums, start, first, diagonal, basis, image, alpha, beta, message
):
    images = image_of(got, column_sums, first, diagonal)
    sums = join_slices(got[:, OWN:, :].reshape(COLUMNS * EXTRA, 128))
    inverse = factor_of(sums)[1]
    alpha_t = dot_t(dot(inverse, pltpu.roll(sums, 128 - K, 1)[:, :K]), inverse)
    image_gram = dot_t(dot(inverse, pltpu.roll(sums, 128 - 2 * K, 1)[:, :K]), inverse)
    wide = jnp.zeros((128 - K, K), f32)
    square = dot_t(alpha_t, jnp.concatenate([alpha_t, wide]))
    upper, inverse_first = factor_of(
        jnp.concatenate([image_gram, jnp.zeros((K, 128 - K), f32)], axis=1) - square
    )
    packed = jnp.zeros((K // 2, 128), f32)
    for block in range(OWN // K):
        where = slice(block * K, (block + 1) * K)
        basis_start = dot(inverse, start[where, :])
        image_start = dot(inverse, first[where, :])
        current = dot(inverse_first, image_start - dot(alpha_t, basis_start))
        moved = dot(inverse, images[block]) - dot(alpha_t, image_start)
        result = dot(inverse_first, moved) - dot(upper, basis_start)
        basis[where, :] = current
        image[where, :] = result
        for half in range(2):
            top = result[half * (K // 2) : (half + 1) * (K // 2), :]
            empty = jnp.zeros_like(result)
            pair = [current, empty, result, empty] if half == 0 else [empty, current, empty, result]
            packed += dot_t(top, jnp.concatenate(pair))
    for device in range(message.shape[0]):
        message[device, :, :] = packed
    alpha[...] = flip(alpha_t)
    beta[...] = flip(upper)


def plane_kernel(got, message):
    total = got[0]
    for device in range(1, got.shape[0]):
        total += got[device]
    for device in range(message.shape[0]):
        message[device, :, :] = total


def last_kernel(scaling, got, basis, image, alpha_first, beta_first, result, alphas, betas):
    total = got[0]
    for device in range(1, got.shape[0]):
        total += got[device]
    turned = [total] + [pltpu.roll(total, 128 - K * place, 1) for place in range(1, 4)]
    alpha_t = jnp.concatenate(turned[:2])[:, :K]
    image_gram = jnp.concatenate(turned[2:])
    wide = jnp.zeros((128 - K, K), f32)
    square = dot_t(alpha_t, jnp.concatenate([alpha_t, wide]))
    upper, inverse = factor_of(image_gram - square)
    for block in range(OWN // K):
        where = slice(block * K, (block + 1) * K)
        residual = image[where, :] - dot(alpha_t, basis[where, :])
        result[where, :] = dot(inverse, residual) * scaling
    alphas[0] = alpha_first[...]
    alphas[1] = flip(alpha_t)
    betas[0] = beta_first[...]
    betas[1] = flip(upper)


def exchange(message, vectors, tiles, lists):
    extra = message.shape[1] - OWN
    got = swap(message, COLUMN)
    sent = call(
        lower_kernel,
        out((NEARS, SLAB + extra, 128), bf16),
        (lists,),
        (got, tiles),
        (pltpu.VMEM((NEARS * SLAB, 128), f32),),
    )
    got = swap(sent, NEAR)
    sent = call(near_kernel, out((FARS, 2 * OWN + extra, 128), bf16), (), (got, vectors))
    got = swap(sent, FAR)
    outs = [out((NEARS, SLAB, 128), bf16), out((OWN, 128), f32)]
    if extra:
        outs.append(out((extra, 128), bf16))
    sent, column_sums, *piece = call(far_kernel, outs, (), (got,))
    got = swap(sent, NEAR)
    sent = call(
        upper_kernel,
        out((COLUMNS, OWN + extra, 128), bf16),
        (lists,),
        (got, tiles, *piece),
        (pltpu.VMEM((COLUMNS * OWN, 128), f32),),
    )
    return swap(sent, COLUMN), column_sums


def local(start_block, tile_values, tile_rows, tile_columns, diagonal_blocks):
    start = start_block.reshape(OWN, 128)
    tiles = tile_values[0, 0]
    matrix = (
        call(stage_kernel, out(tiles.shape, bf16), (), (tiles,)),
        jnp.concatenate([tile_rows[0, 0], tile_columns[0, 0]]),
    )
    vectors = out((OWN, 128), f32)
    square = out((K, K), f32)
    message = call(prepare_kernel, out((COLUMNS, OWN, 128), bf16), (), (start,))
    got, column_sums = exchange(message, start, *matrix)
    first, message = call(
        middle_kernel,
        (vectors, out((COLUMNS, OWN + EXTRA, 128), bf16)),
        (),
        (got, column_sums, start, diagonal_blocks),
    )
    got, column_sums = exchange(message, first, *matrix)
    planes, depths = lax.axis_size(PLANE), lax.axis_size(DEPTH)
    basis, image, alpha_first, beta_first, message = call(
        finish_kernel,
        (vectors, vectors, square, square, out((planes, K // 2, 128), f32)),
        (),
        (got, column_sums, start, first, diagonal_blocks),
    )
    got = swap(message, PLANE)
    message = call(plane_kernel, out((depths, K // 2, 128), f32), (), (got,))
    got = swap(message, DEPTH)
    scaling = math.sqrt(start_block.shape[0] * start_block.shape[2] * planes * depths)
    pair = out((2, K, K), f32)
    result, alphas, betas = call(
        functools.partial(last_kernel, scaling),
        (vectors, pair, pair),
        (),
        (got, basis, image, alpha_first, beta_first),
    )
    return result.reshape(start_block.shape), alphas, betas


def solution(mesh):
    split = Mesh(mesh.devices.reshape(2, FARS, 2, 2, 4, 2), AXES)
    rows = ("x_high", "far", "near")
    owner = P((*COLUMN, *rows), None, None)
    placed = (
        owner,
        P(rows, COLUMN, None, None, None),
        P(rows, COLUMN, None),
        P(rows, COLUMN, None),
        owner,
    )
    return jax.shard_map(
        local,
        mesh=split,
        in_specs=placed,
        out_specs=(owner, P(), P()),
        check_vma=False,
    )
```

```python
import functools
import math

import jax
import jax.numpy as jnp
from jax import lax
from jax.experimental import pallas as pl
from jax.experimental.pallas import tpu as pltpu
from jax.sharding import Mesh
from jax.sharding import PartitionSpec as P

AXES = ("x_high", "far", "near", "x_low", "y", "core")
COLUMN = ("x_low", "y", "core")
PLANE = ("x_high", *COLUMN)
DEPTH = ("far", "near")
NEAR = ("x_high", "near")
FAR = ("far",)

NEARS = 4
FARS = 8
COLUMNS = 16
K = 32
OWN = 64
SLAB = FARS * OWN
EXTRA = 16
TERMS = 3
GROUP = 8
PANEL = 8

highest = lax.Precision.HIGHEST
f32 = jnp.float32
bf16 = jnp.bfloat16


def swap(parts, axis):
    return lax.all_to_all(parts, axis, 0, 0, tiled=True)


def call(kernel, outs, scalars, arrays, scratch=()):
    specs = [pl.BlockSpec(memory_space=pltpu.SMEM)] * len(scalars)
    specs += [pl.BlockSpec(memory_space=pltpu.VMEM)] * len(arrays)
    return pl.pallas_call(
        kernel,
        out_shape=outs,
        in_specs=specs,
        out_specs=jax.tree.map(lambda _: pl.BlockSpec(memory_space=pltpu.VMEM), outs),
        scratch_shapes=list(scratch),
        compiler_params=pltpu.CompilerParams(vmem_limit_bytes=16 * 2**20),
    )(*scalars, *arrays)


def out(shape, dtype):
    return jax.ShapeDtypeStruct(shape, dtype)


def iota(shape, dimension):
    return lax.broadcasted_iota(jnp.int32, shape, dimension)


def dot(left, right):
    return jnp.dot(left, right, precision=highest, preferred_element_type=f32)


def dot_t(left, right, precision=highest):
    return lax.dot_general(
        left, right, (((1,), (1,)), ((), ())), precision=precision, preferred_element_type=f32
    )


def terms_of(values):
    high = values.astype(bf16)
    rest = values - high.astype(f32)
    middle = rest.astype(bf16)
    low = (rest - middle.astype(f32)).astype(bf16)
    return high, middle, low


def one_hot(condition):
    return jnp.where(condition, 1.0, 0.0).astype(bf16)


def spread_slices(grams):
    source = jnp.concatenate(terms_of(grams), axis=0)
    shape = (COLUMNS * EXTRA, TERMS * K)
    row, column = iota(shape, 0), iota(shape, 1)
    place = row & (EXTRA - 1)
    wanted = (place >> 1) * K + (row >> 4) * 2 + (place & 1)
    picker = one_hot((place < 2 * TERMS) & (column == wanted))
    return jnp.dot(picker, source, preferred_element_type=f32).astype(bf16)


def sum_slices(pieces):
    shape = (EXTRA, pieces.shape[0])
    row, column = iota(shape, 0), iota(shape, 1)
    picker = one_hot(((column & 15) < 2 * TERMS) & ((column & 1) == (row & 1)))
    total = jnp.dot(picker, pieces, preferred_element_type=f32)
    high, middle, low = (term.astype(f32) for term in terms_of(total))
    place = iota(total.shape, 0)
    chosen = jnp.where(place < 2, high, jnp.where(place < 4, middle, low))
    return jnp.where(place < 2 * TERMS, chosen, 0.0).astype(bf16)


def join_slices(pieces):
    shape = (K, pieces.shape[0])
    row, column = iota(shape, 0), iota(shape, 1)
    picker = one_hot(
        ((column >> 4) == (row >> 1)) & ((column & 15) < 2 * TERMS) & ((column & 1) == (row & 1))
    )
    return jnp.dot(picker, pieces, preferred_element_type=f32)


def eliminate(gram):
    count = gram.shape[0]
    shape = (count, 128)
    row, column = iota(shape, 0), iota(shape, 1)
    work = jnp.where(column < count, gram, jnp.where(column == row + count, 1.0, 0.0))
    for base in range(0, count, PANEL):
        columns = [
            jnp.broadcast_to(work[:, base + step : base + step + 1], shape) for step in range(PANEL)
        ]
        leads = [work[base + step : base + step + 1, :] for step in range(PANEL)]
        for step in range(PANEL):
            scale = lax.rsqrt(columns[step][base + step : base + step + 1, :])
            columns[step] *= scale
            leads[step] *= scale
            for later in range(step + 1, PANEL):
                share = columns[step][base + later : base + later + 1, :]
                columns[later] -= columns[step] * share
                leads[later] -= leads[step] * share
        lower = work
        for step in range(PANEL):
            lower -= columns[step] * leads[step]
        work = jnp.where(row >= base + PANEL, lower, work)
        for step in range(PANEL):
            work = jnp.where(row == base + step, leads[step], work)
    return work


def lanes(matrix, place):
    return (pltpu.roll(matrix, 128 - K * place, 1) if place else matrix)[:, :K]


def upper_part(matrix):
    return jnp.where(iota((K, K), 1) >= iota((K, K), 0), matrix, 0.0)


def flip(matrix):
    eye = jnp.where(iota((K, K), 0) == iota((K, K), 1), 1.0, 0.0)
    return dot_t(eye, matrix)


def fill(message, rows):
    for device in range(message.shape[0]):
        message[device, : rows.shape[0], :] = rows


def stage_kernel(tiles, staged, turned):
    for tile in range(tiles.shape[0]):
        staged[tile] = tiles[tile]
        turned[tile] = tiles[tile].T


def prepare_kernel(start, message):
    fill(message, start[...].astype(bf16))


def lower_kernel(lists, got, tiles, message, total):
    total[...] = jnp.zeros_like(total)
    count = tiles.shape[0]
    for base in range(0, count, GROUP):
        parts = []
        for tile in range(base, base + GROUP):
            place = lists[tile]
            vectors = got[place >> 1, pl.ds(pl.multiple_of((place & 1) * K, K), K), :]
            parts.append(jnp.dot(vectors, tiles[tile], preferred_element_type=f32))
        for tile in range(base, base + GROUP):
            place = lists[count + tile]
            owner = place >> 1
            near = (owner >> 4) * 2 + (owner & 1)
            spot = (near * FARS + ((owner >> 1) & 7)) * 2 + (place & 1)
            where = pl.ds(pl.multiple_of(spot * K, K), K)
            total[where, :] += parts[tile - base]
    message[:, :SLAB, :] = total[...].astype(bf16).reshape(NEARS, SLAB, 128)
    if got.shape[1] > OWN:
        piece = sum_slices(got[:, OWN:, :].reshape(COLUMNS * EXTRA, 128))
        for device in range(NEARS):
            message[device, SLAB:, :] = piece


def near_kernel(got, vectors, message):
    total = got[0, :SLAB, :].astype(f32)
    for device in range(1, NEARS):
        total += got[device, :SLAB, :].astype(f32)
    message[:, OWN : 2 * OWN, :] = total.astype(bf16).reshape(FARS, OWN, 128)
    fill(message, vectors[...].astype(bf16))
    if got.shape[1] > SLAB:
        piece = sum_slices(got[:, SLAB:, :].reshape(NEARS * EXTRA, 128))
        for device in range(FARS):
            message[device, 2 * OWN :, :] = piece


def far_kernel(got, message, column_sums, *piece):
    total = got[0, OWN : 2 * OWN, :].astype(f32)
    for device in range(1, FARS):
        total += got[device, OWN : 2 * OWN, :].astype(f32)
    column_sums[...] = total
    if piece:
        piece[0][...] = sum_slices(got[:, 2 * OWN :, :].reshape(FARS * EXTRA, 128))
    fill(message, got[:, :OWN, :].reshape(SLAB, 128))


def upper_kernel(lists, got, tiles, *refs):
    *piece, message, total = refs
    total[...] = jnp.zeros_like(total)
    count = tiles.shape[0]
    for base in range(0, count, GROUP):
        parts = []
        for tile in range(base, base + GROUP):
            place = lists[count + tile]
            owner = place >> 1
            near = (owner >> 4) * 2 + (owner & 1)
            spot = ((owner >> 1) & 7) * 2 + (place & 1)
            vectors = got[near, pl.ds(pl.multiple_of(spot * K, K), K), :]
            parts.append(jnp.dot(vectors, tiles[tile], preferred_element_type=f32))
        for tile in range(base, base + GROUP):
            where = pl.ds(pl.multiple_of(lists[tile] * K, K), K)
            total[where, :] += parts[tile - base]
    message[:, :OWN, :] = total[...].astype(bf16).reshape(COLUMNS, OWN, 128)
    if piece:
        for device in range(COLUMNS):
            message[device, OWN:, :] = piece[0][...]


def image_of(got, column_sums, vectors, diagonal):
    images = []
    for block in range(OWN // K):
        where = slice(block * K, (block + 1) * K)
        narrow = vectors[where, :].astype(bf16)
        image = dot_t(narrow, diagonal[block], None)
        image += jnp.dot(narrow, diagonal[block], preferred_element_type=f32)
        image = 0.5 * image + column_sums[where, :]
        total = got[0, where, :].astype(f32)
        for device in range(1, COLUMNS):
            total += got[device, where, :].astype(f32)
        images.append(image + total)
    return images


def middle_kernel(got, column_sums, start, diagonal, image, message):
    images = image_of(got, column_sums, start, diagonal)
    grams = jnp.zeros((K, 128), f32)
    empty = jnp.zeros((K, 128), f32)
    for block in range(OWN // K):
        where = slice(block * K, (block + 1) * K)
        vectors = start[where, :]
        image[where, :] = images[block]
        pair = [vectors, images[block]]
        grams += dot_t(vectors, jnp.concatenate(pair + [empty, empty]))
        grams += dot_t(images[block], jnp.concatenate([empty, empty] + pair))
    fill(message, jnp.concatenate(images).astype(bf16))
    message[:, OWN:, :] = spread_slices(grams).reshape(COLUMNS, EXTRA, 128)


def finish_kernel(
    got, column_sums, start, first, diagonal, basis, image, alpha, beta, message
):
    images = image_of(got, column_sums, first, diagonal)
    sums = join_slices(got[:, OWN:, :].reshape(COLUMNS * EXTRA, 128))
    work = eliminate(jnp.concatenate([sums, pltpu.roll(sums, 128 - 2 * K, 1)]))
    upper = upper_part(lanes(work[K:], 1))
    inverse = lanes(work[:K], 2)
    weights = pltpu.roll(work[K:], 128 - 2 * K, 1)[:, : 2 * K]
    back = dot(dot_t(upper, inverse), inverse)
    packed = jnp.zeros((K // 2, 128), f32)
    for block in range(OWN // K):
        where = slice(block * K, (block + 1) * K)
        current = dot(weights, jnp.concatenate([start[where, :], first[where, :]]))
        result = dot(weights, jnp.concatenate([first[where, :], images[block]]))
        result -= dot(back, start[where, :])
        basis[where, :] = current
        image[where, :] = result
        for half in range(2):
            top = result[half * (K // 2) : (half + 1) * (K // 2), :]
            empty = jnp.zeros_like(result)
            pair = [current, empty, result, empty] if half == 0 else [empty, current, empty, result]
            packed += dot_t(top, jnp.concatenate(pair))
    for device in range(message.shape[0]):
        message[device, :, :] = packed
    alpha[...] = dot_t(lanes(work[:K], 1), inverse)
    beta[...] = dot_t(inverse, upper)


def plane_kernel(got, message):
    total = got[0]
    for device in range(1, got.shape[0]):
        total += got[device]
    for device in range(message.shape[0]):
        message[device, :, :] = total


def last_kernel(scaling, got, basis, image, alpha_first, beta_first, result, alphas, betas):
    total = got[0]
    for device in range(1, got.shape[0]):
        total += got[device]
    turned = [total] + [pltpu.roll(total, 128 - K * place, 1) for place in range(1, 4)]
    alpha_t = jnp.concatenate(turned[:2])[:, :K]
    image_gram = jnp.concatenate(turned[2:])
    wide = jnp.zeros((128 - K, K), f32)
    square = dot_t(alpha_t, jnp.concatenate([alpha_t, wide]))
    work = eliminate(image_gram - square)
    upper, inverse = upper_part(work[:, :K]), lanes(work, 1)
    for block in range(OWN // K):
        where = slice(block * K, (block + 1) * K)
        residual = image[where, :] - dot(alpha_t, basis[where, :])
        result[where, :] = dot(inverse, residual) * scaling
    alphas[0] = alpha_first[...]
    alphas[1] = flip(alpha_t)
    betas[0] = beta_first[...]
    betas[1] = flip(upper)


def exchange(message, vectors, tiles, turned, lists):
    extra = message.shape[1] - OWN
    got = swap(message, COLUMN)
    sent = call(
        lower_kernel,
        out((NEARS, SLAB + extra, 128), bf16),
        (lists,),
        (got, tiles),
        (pltpu.VMEM((NEARS * SLAB, 128), f32),),
    )
    got = swap(sent, NEAR)
    sent = call(near_kernel, out((FARS, 2 * OWN + extra, 128), bf16), (), (got, vectors))
    got = swap(sent, FAR)
    outs = [out((NEARS, SLAB, 128), bf16), out((OWN, 128), f32)]
    if extra:
        outs.append(out((extra, 128), bf16))
    sent, column_sums, *piece = call(far_kernel, outs, (), (got,))
    got = swap(sent, NEAR)
    sent = call(
        upper_kernel,
        out((COLUMNS, OWN + extra, 128), bf16),
        (lists,),
        (got, turned, *piece),
        (pltpu.VMEM((COLUMNS * OWN, 128), f32),),
    )
    return swap(sent, COLUMN), column_sums


def local(start_block, tile_values, tile_rows, tile_columns, diagonal_blocks):
    start = start_block.reshape(OWN, 128)
    tiles = tile_values[0, 0]
    matrix = (
        *call(stage_kernel, (out(tiles.shape, bf16), out(tiles.shape, bf16)), (), (tiles,)),
        jnp.concatenate([tile_rows[0, 0], tile_columns[0, 0]]),
    )
    vectors = out((OWN, 128), f32)
    square = out((K, K), f32)
    message = call(prepare_kernel, out((COLUMNS, OWN, 128), bf16), (), (start,))
    got, column_sums = exchange(message, start, *matrix)
    first, message = call(
        middle_kernel,
        (vectors, out((COLUMNS, OWN + EXTRA, 128), bf16)),
        (),
        (got, column_sums, start, diagonal_blocks),
    )
    got, column_sums = exchange(message, first, *matrix)
    planes, depths = lax.axis_size(PLANE), lax.axis_size(DEPTH)
    basis, image, alpha_first, beta_first, message = call(
        finish_kernel,
        (vectors, vectors, square, square, out((planes, K // 2, 128), f32)),
        (),
        (got, column_sums, start, first, diagonal_blocks),
    )
    got = swap(message, PLANE)
    message = call(plane_kernel, out((depths, K // 2, 128), f32), (), (got,))
    got = swap(message, DEPTH)
    scaling = math.sqrt(start_block.shape[0] * start_block.shape[2] * planes * depths)
    pair = out((2, K, K), f32)
    result, alphas, betas = call(
        functools.partial(last_kernel, scaling),
        (vectors, pair, pair),
        (),
        (got, basis, image, alpha_first, beta_first),
    )
    return result.reshape(start_block.shape), alphas, betas


def solution(mesh):
    split = Mesh(mesh.devices.reshape(2, FARS, 2, 2, 4, 2), AXES)
    rows = ("x_high", "far", "near")
    owner = P((*COLUMN, *rows), None, None)
    placed = (
        owner,
        P(rows, COLUMN, None, None, None),
        P(rows, COLUMN, None),
        P(rows, COLUMN, None),
        owner,
    )
    return jax.shard_map(
        local,
        mesh=split,
        in_specs=placed,
        out_specs=(owner, P(), P()),
        check_vma=False,
    )
```

```python
import functools
import math

import jax
import jax.numpy as jnp
from jax import lax
from jax.experimental import pallas as pl
from jax.experimental.pallas import tpu as pltpu
from jax.sharding import Mesh
from jax.sharding import PartitionSpec as P

AXES = ("x_high", "far", "near", "x_low", "y", "core")
COLUMN = ("x_low", "y", "core")
PLANE = ("x_high", *COLUMN)
DEPTH = ("far", "near")
NEAR = ("x_high", "near")
FAR = ("far",)

NEARS = 4
FARS = 8
COLUMNS = 16
K = 32
OWN = 64
SLAB = FARS * OWN
EXTRA = 16
TERMS = 3
GROUP = 8
PANEL = 8
PACKED = K * K + 128

highest = lax.Precision.HIGHEST
f32 = jnp.float32
bf16 = jnp.bfloat16


def swap(parts, axis):
    return lax.all_to_all(parts, axis, 0, 0, tiled=True)


def call(kernel, outs, scalars, arrays, scratch=()):
    specs = [pl.BlockSpec(memory_space=pltpu.SMEM)] * len(scalars)
    specs += [pl.BlockSpec(memory_space=pltpu.VMEM)] * len(arrays)
    return pl.pallas_call(
        kernel,
        out_shape=outs,
        in_specs=specs,
        out_specs=jax.tree.map(lambda _: pl.BlockSpec(memory_space=pltpu.VMEM), outs),
        scratch_shapes=list(scratch),
        compiler_params=pltpu.CompilerParams(vmem_limit_bytes=16 * 2**20),
    )(*scalars, *arrays)


def out(shape, dtype):
    return jax.ShapeDtypeStruct(shape, dtype)


def iota(shape, dimension):
    return lax.broadcasted_iota(jnp.int32, shape, dimension)


def dot(left, right):
    return jnp.dot(left, right, precision=highest, preferred_element_type=f32)


def dot_t(left, right, precision=highest):
    return lax.dot_general(
        left, right, (((1,), (1,)), ((), ())), precision=precision, preferred_element_type=f32
    )


def terms_of(values):
    high = values.astype(bf16)
    rest = values - high.astype(f32)
    middle = rest.astype(bf16)
    low = (rest - middle.astype(f32)).astype(bf16)
    return high, middle, low


def one_hot(condition):
    return jnp.where(condition, 1.0, 0.0).astype(bf16)


def spread_slices(grams):
    source = jnp.concatenate(terms_of(grams), axis=0)
    shape = (COLUMNS * EXTRA, TERMS * K)
    row, column = iota(shape, 0), iota(shape, 1)
    place = row & (EXTRA - 1)
    wanted = (place >> 1) * K + (row >> 4) * 2 + (place & 1)
    picker = one_hot((place < 2 * TERMS) & (column == wanted))
    return jnp.dot(picker, source, preferred_element_type=f32).astype(bf16)


def sum_slices(pieces):
    shape = (EXTRA, pieces.shape[0])
    row, column = iota(shape, 0), iota(shape, 1)
    picker = one_hot(((column & 15) < 2 * TERMS) & ((column & 1) == (row & 1)))
    total = jnp.dot(picker, pieces, preferred_element_type=f32)
    high, middle, low = (term.astype(f32) for term in terms_of(total))
    place = iota(total.shape, 0)
    chosen = jnp.where(place < 2, high, jnp.where(place < 4, middle, low))
    return jnp.where(place < 2 * TERMS, chosen, 0.0).astype(bf16)


def join_slices(pieces):
    shape = (K, pieces.shape[0])
    row, column = iota(shape, 0), iota(shape, 1)
    picker = one_hot(
        ((column >> 4) == (row >> 1)) & ((column & 15) < 2 * TERMS) & ((column & 1) == (row & 1))
    )
    return jnp.dot(picker, pieces, preferred_element_type=f32)


def eliminate(gram):
    count = gram.shape[0]
    shape = (count, 128)
    row, column = iota(shape, 0), iota(shape, 1)
    work = jnp.where(column < count, gram, jnp.where(column == row + count, 1.0, 0.0))
    for base in range(0, count, PANEL):
        columns = [
            jnp.broadcast_to(work[:, base + step : base + step + 1], shape) for step in range(PANEL)
        ]
        leads = [work[base + step : base + step + 1, :] for step in range(PANEL)]
        for step in range(PANEL):
            scale = lax.rsqrt(columns[step][base + step : base + step + 1, :])
            columns[step] *= scale
            leads[step] *= scale
            for later in range(step + 1, PANEL):
                share = columns[step][base + later : base + later + 1, :]
                columns[later] -= columns[step] * share
                leads[later] -= leads[step] * share
        lower = work
        for step in range(PANEL):
            lower -= columns[step] * leads[step]
        work = jnp.where(row >= base + PANEL, lower, work)
        for step in range(PANEL):
            work = jnp.where(row == base + step, leads[step], work)
    return work


def lanes(matrix, place):
    return (pltpu.roll(matrix, 128 - K * place, 1) if place else matrix)[:, :K]


def upper_part(matrix):
    return jnp.where(iota((K, K), 1) >= iota((K, K), 0), matrix, 0.0)


def flip(matrix):
    eye = jnp.where(iota((K, K), 0) == iota((K, K), 1), 1.0, 0.0)
    return dot_t(eye, matrix)


def fill(message, rows):
    for device in range(message.shape[0]):
        message[device, : rows.shape[0], :] = rows


def stage_kernel(tiles, staged, turned):
    for tile in range(tiles.shape[0]):
        staged[tile] = tiles[tile]
        turned[tile] = tiles[tile].T


def pack(square, cross):
    row, column = iota((K, 128), 0), iota((K, 128), 1)
    both = jnp.where(column < K, jnp.where(row >= column, square, cross), 0.0)
    quarter = K // 4
    folded = both[:quarter]
    for place in range(1, 4):
        folded += pltpu.roll(both[place * quarter : (place + 1) * quarter], K * place, 1)
    middle = jnp.sum(jnp.where(row == column, cross, 0.0), axis=0, keepdims=True)
    return jnp.concatenate([folded[line : line + 1] for line in range(quarter)] + [middle], axis=1)


def unpack(packed):
    quarter = K // 4
    folded = jnp.concatenate([packed[:, 128 * line : 128 * (line + 1)] for line in range(quarter)])
    both = jnp.concatenate([lanes(folded, place) for place in range(4)])
    other = flip(both)
    row, column = iota((K, K), 0), iota((K, K), 1)
    square = jnp.where(row >= column, both, other)
    middle = packed[:, 128 * quarter : 128 * quarter + K]
    cross = jnp.where(row < column, both, jnp.where(row == column, middle, other))
    return square, cross


def lower_kernel(lists, got, tiles, message, total):
    total[...] = jnp.zeros_like(total)
    count = tiles.shape[0]
    for base in range(0, count, GROUP):
        parts = []
        for tile in range(base, base + GROUP):
            place = lists[tile]
            vectors = got[place >> 1, pl.ds(pl.multiple_of((place & 1) * K, K), K), :]
            parts.append(jnp.dot(vectors, tiles[tile], preferred_element_type=f32))
        for tile in range(base, base + GROUP):
            place = lists[count + tile]
            owner = place >> 1
            near = (owner >> 4) * 2 + (owner & 1)
            spot = (near * FARS + ((owner >> 1) & 7)) * 2 + (place & 1)
            where = pl.ds(pl.multiple_of(spot * K, K), K)
            total[where, :] += parts[tile - base]
    message[:, :SLAB, :] = total[...].astype(bf16).reshape(NEARS, SLAB, 128)
    if got.shape[1] > OWN:
        piece = sum_slices(got[:, OWN:, :].reshape(COLUMNS * EXTRA, 128))
        for device in range(NEARS):
            message[device, SLAB:, :] = piece


def near_kernel(got, vectors, message):
    total = got[0, :SLAB, :].astype(f32)
    for device in range(1, NEARS):
        total += got[device, :SLAB, :].astype(f32)
    message[:, OWN : 2 * OWN, :] = total.astype(bf16).reshape(FARS, OWN, 128)
    fill(message, vectors[...].astype(bf16))
    if got.shape[1] > SLAB:
        piece = sum_slices(got[:, SLAB:, :].reshape(NEARS * EXTRA, 128))
        for device in range(FARS):
            message[device, 2 * OWN :, :] = piece


def far_kernel(got, message, column_sums, *piece):
    total = got[0, OWN : 2 * OWN, :].astype(f32)
    for device in range(1, FARS):
        total += got[device, OWN : 2 * OWN, :].astype(f32)
    column_sums[...] = total
    if piece:
        piece[0][...] = sum_slices(got[:, 2 * OWN :, :].reshape(FARS * EXTRA, 128))
    fill(message, got[:, :OWN, :].reshape(SLAB, 128))


def upper_kernel(lists, got, tiles, *refs):
    *piece, message, total = refs
    total[...] = jnp.zeros_like(total)
    count = tiles.shape[0]
    for base in range(0, count, GROUP):
        parts = []
        for tile in range(base, base + GROUP):
            place = lists[count + tile]
            owner = place >> 1
            near = (owner >> 4) * 2 + (owner & 1)
            spot = ((owner >> 1) & 7) * 2 + (place & 1)
            vectors = got[near, pl.ds(pl.multiple_of(spot * K, K), K), :]
            parts.append(jnp.dot(vectors, tiles[tile], preferred_element_type=f32))
        for tile in range(base, base + GROUP):
            where = pl.ds(pl.multiple_of(lists[tile] * K, K), K)
            total[where, :] += parts[tile - base]
    message[:, :OWN, :] = total[...].astype(bf16).reshape(COLUMNS, OWN, 128)
    if piece:
        for device in range(COLUMNS):
            message[device, OWN:, :] = piece[0][...]


def image_of(got, column_sums, vectors, diagonal):
    images = []
    for block in range(OWN // K):
        where = slice(block * K, (block + 1) * K)
        narrow = vectors[where, :].astype(bf16)
        image = dot_t(narrow, diagonal[block], None)
        image += jnp.dot(narrow, diagonal[block], preferred_element_type=f32)
        image = 0.5 * image + column_sums[where, :]
        total = got[0, where, :].astype(f32)
        for device in range(1, COLUMNS):
            total += got[device, where, :].astype(f32)
        images.append(image + total)
    return images


def middle_kernel(got, column_sums, start, diagonal, image, message):
    images = image_of(got, column_sums, start, diagonal)
    grams = jnp.zeros((K, 128), f32)
    empty = jnp.zeros((K, 128), f32)
    for block in range(OWN // K):
        where = slice(block * K, (block + 1) * K)
        vectors = start[where, :]
        image[where, :] = images[block]
        pair = [vectors, images[block]]
        grams += dot_t(vectors, jnp.concatenate(pair + [empty, empty]))
        grams += dot_t(images[block], jnp.concatenate([empty, empty] + pair))
    fill(message, jnp.concatenate(images).astype(bf16))
    message[:, OWN:, :] = spread_slices(grams).reshape(COLUMNS, EXTRA, 128)


def finish_kernel(
    got, column_sums, start, first, diagonal, basis, image, alpha, beta, message
):
    images = image_of(got, column_sums, first, diagonal)
    sums = join_slices(got[:, OWN:, :].reshape(COLUMNS * EXTRA, 128))
    work = eliminate(jnp.concatenate([sums, pltpu.roll(sums, 128 - 2 * K, 1)]))
    upper = upper_part(lanes(work[K:], 1))
    inverse = lanes(work[:K], 2)
    weights = pltpu.roll(work[K:], 128 - 2 * K, 1)[:, : 2 * K]
    back = dot(dot_t(upper, inverse), inverse)
    square = jnp.zeros((K, 128), f32)
    cross = jnp.zeros((K, 128), f32)
    empty = [jnp.zeros((K, 128), f32)] * 3
    for block in range(OWN // K):
        where = slice(block * K, (block + 1) * K)
        current = dot(weights, jnp.concatenate([start[where, :], first[where, :]]))
        result = dot(weights, jnp.concatenate([first[where, :], images[block]]))
        result -= dot(back, start[where, :])
        basis[where, :] = current
        image[where, :] = result
        wide = jnp.concatenate([result] + empty)
        square += dot_t(result, wide)
        cross += dot_t(current, wide)
    packed = pack(square, cross)
    for device in range(message.shape[0]):
        message[device] = packed
    alpha[...] = dot_t(lanes(work[:K], 1), inverse)
    beta[...] = dot_t(inverse, upper)


def plane_kernel(got, message):
    total = got[0]
    for device in range(1, got.shape[0]):
        total += got[device]
    for device in range(message.shape[0]):
        message[device, :, :] = total


def last_kernel(scaling, got, basis, image, alpha_first, beta_first, result, alphas, betas):
    total = got[0]
    for device in range(1, got.shape[0]):
        total += got[device]
    image_gram, alpha_last = unpack(total)
    wide = jnp.zeros((K, 128 - K), f32)
    work = eliminate(jnp.concatenate([image_gram - dot(alpha_last, alpha_last), wide], axis=1))
    upper, inverse = upper_part(work[:, :K]), lanes(work, 1)
    for block in range(OWN // K):
        where = slice(block * K, (block + 1) * K)
        residual = image[where, :] - dot(alpha_last, basis[where, :])
        result[where, :] = dot(inverse, residual) * scaling
    alphas[0] = alpha_first[...]
    alphas[1] = alpha_last
    betas[0] = beta_first[...]
    betas[1] = flip(upper)


def exchange(message, vectors, tiles, turned, lists):
    extra = message.shape[1] - OWN
    got = swap(message, COLUMN)
    sent = call(
        lower_kernel,
        out((NEARS, SLAB + extra, 128), bf16),
        (lists,),
        (got, tiles),
        (pltpu.VMEM((NEARS * SLAB, 128), f32),),
    )
    got = swap(sent, NEAR)
    sent = call(near_kernel, out((FARS, 2 * OWN + extra, 128), bf16), (), (got, vectors))
    got = swap(sent, FAR)
    outs = [out((NEARS, SLAB, 128), bf16), out((OWN, 128), f32)]
    if extra:
        outs.append(out((extra, 128), bf16))
    sent, column_sums, *piece = call(far_kernel, outs, (), (got,))
    got = swap(sent, NEAR)
    sent = call(
        upper_kernel,
        out((COLUMNS, OWN + extra, 128), bf16),
        (lists,),
        (got, turned, *piece),
        (pltpu.VMEM((COLUMNS * OWN, 128), f32),),
    )
    return swap(sent, COLUMN), column_sums


def local(start_block, tile_values, tile_rows, tile_columns, diagonal_blocks):
    start = start_block.reshape(OWN, 128)
    tiles = tile_values[0, 0]
    matrix = (
        *call(stage_kernel, (out(tiles.shape, bf16), out(tiles.shape, bf16)), (), (tiles,)),
        jnp.concatenate([tile_rows[0, 0], tile_columns[0, 0]]),
    )
    vectors = out((OWN, 128), f32)
    square = out((K, K), f32)
    message = jnp.broadcast_to(start.astype(bf16), (COLUMNS, OWN, 128))
    got, column_sums = exchange(message, start, *matrix)
    first, message = call(
        middle_kernel,
        (vectors, out((COLUMNS, OWN + EXTRA, 128), bf16)),
        (),
        (got, column_sums, start, diagonal_blocks),
    )
    got, column_sums = exchange(message, first, *matrix)
    planes, depths = lax.axis_size(PLANE), lax.axis_size(DEPTH)
    basis, image, alpha_first, beta_first, message = call(
        finish_kernel,
        (vectors, vectors, square, square, out((planes, 1, PACKED), f32)),
        (),
        (got, column_sums, start, first, diagonal_blocks),
    )
    got = swap(message, PLANE)
    message = call(plane_kernel, out((depths, 1, PACKED), f32), (), (got,))
    got = swap(message, DEPTH)
    scaling = math.sqrt(start_block.shape[0] * start_block.shape[2] * planes * depths)
    pair = out((2, K, K), f32)
    result, alphas, betas = call(
        functools.partial(last_kernel, scaling),
        (vectors, pair, pair),
        (),
        (got, basis, image, alpha_first, beta_first),
    )
    return result.reshape(start_block.shape), alphas, betas


def solution(mesh):
    split = Mesh(mesh.devices.reshape(2, FARS, 2, 2, 4, 2), AXES)
    rows = ("x_high", "far", "near")
    owner = P((*COLUMN, *rows), None, None)
    placed = (
        owner,
        P(rows, COLUMN, None, None, None),
        P(rows, COLUMN, None),
        P(rows, COLUMN, None),
        owner,
    )
    return jax.shard_map(
        local,
        mesh=split,
        in_specs=placed,
        out_specs=(owner, P(), P()),
        check_vma=False,
    )
```

```python
import functools
import math

import jax
import jax.numpy as jnp
from jax import lax
from jax.experimental import pallas as pl
from jax.experimental.pallas import tpu as pltpu
from jax.sharding import Mesh
from jax.sharding import PartitionSpec as P

AXES = ("x_high", "far", "near", "x_low", "y", "core")
COLUMN = ("x_low", "y", "core")
PLANE = ("x_high", *COLUMN)
DEPTH = ("far", "near")
NEAR = ("x_high", "near")
FAR = ("far",)

NEARS = 4
FARS = 8
COLUMNS = 16
K = 32
OWN = 64
SLAB = FARS * OWN
EXTRA = 16
TERMS = 3
GROUP = 8
PANEL = 16
PACKED = K * K + 128

highest = lax.Precision.HIGHEST
f32 = jnp.float32
bf16 = jnp.bfloat16


def swap(parts, axis):
    return lax.all_to_all(parts, axis, 0, 0, tiled=True)


def call(kernel, outs, scalars, arrays, scratch=()):
    specs = [pl.BlockSpec(memory_space=pltpu.SMEM)] * len(scalars)
    specs += [pl.BlockSpec(memory_space=pltpu.VMEM)] * len(arrays)
    return pl.pallas_call(
        kernel,
        out_shape=outs,
        in_specs=specs,
        out_specs=jax.tree.map(lambda _: pl.BlockSpec(memory_space=pltpu.VMEM), outs),
        scratch_shapes=list(scratch),
        compiler_params=pltpu.CompilerParams(vmem_limit_bytes=16 * 2**20),
    )(*scalars, *arrays)


def out(shape, dtype):
    return jax.ShapeDtypeStruct(shape, dtype)


def iota(shape, dimension):
    return lax.broadcasted_iota(jnp.int32, shape, dimension)


def dot(left, right):
    return jnp.dot(left, right, precision=highest, preferred_element_type=f32)


def dot_t(left, right, precision=highest):
    return lax.dot_general(
        left, right, (((1,), (1,)), ((), ())), precision=precision, preferred_element_type=f32
    )


def terms_of(values):
    high = values.astype(bf16)
    rest = values - high.astype(f32)
    middle = rest.astype(bf16)
    low = (rest - middle.astype(f32)).astype(bf16)
    return high, middle, low


def one_hot(condition):
    return jnp.where(condition, 1.0, 0.0).astype(bf16)


def spread_slices(grams):
    source = jnp.concatenate(terms_of(grams), axis=0)
    shape = (COLUMNS * EXTRA, TERMS * K)
    row, column = iota(shape, 0), iota(shape, 1)
    place = row & (EXTRA - 1)
    wanted = (place >> 1) * K + (row >> 4) * 2 + (place & 1)
    picker = one_hot((place < 2 * TERMS) & (column == wanted))
    return jnp.dot(picker, source, preferred_element_type=f32).astype(bf16)


def sum_slices(pieces):
    shape = (EXTRA, pieces.shape[0])
    row, column = iota(shape, 0), iota(shape, 1)
    picker = one_hot(((column & 15) < 2 * TERMS) & ((column & 1) == (row & 1)))
    total = jnp.dot(picker, pieces, preferred_element_type=f32)
    high, middle, low = (term.astype(f32) for term in terms_of(total))
    place = iota(total.shape, 0)
    chosen = jnp.where(place < 2, high, jnp.where(place < 4, middle, low))
    return jnp.where(place < 2 * TERMS, chosen, 0.0).astype(bf16)


def join_slices(pieces):
    shape = (K, pieces.shape[0])
    row, column = iota(shape, 0), iota(shape, 1)
    picker = one_hot(
        ((column >> 4) == (row >> 1)) & ((column & 15) < 2 * TERMS) & ((column & 1) == (row & 1))
    )
    return jnp.dot(picker, pieces, preferred_element_type=f32)


def eliminate(gram):
    count = gram.shape[0]
    shape = (count, 128)
    row, column = iota(shape, 0), iota(shape, 1)
    work = jnp.where(column < count, gram, jnp.where(column == row + count, 1.0, 0.0))
    for base in range(0, count, PANEL):
        columns = [
            jnp.broadcast_to(work[:, base + step : base + step + 1], shape) for step in range(PANEL)
        ]
        leads = [work[base + step : base + step + 1, :] for step in range(PANEL)]
        for step in range(PANEL):
            scale = lax.rsqrt(columns[step][base + step : base + step + 1, :])
            columns[step] *= scale
            leads[step] *= scale
            for later in range(step + 1, PANEL):
                share = columns[step][base + later : base + later + 1, :]
                columns[later] -= columns[step] * share
                leads[later] -= leads[step] * share
        lower = work
        for step in range(PANEL):
            lower -= columns[step] * leads[step]
        work = jnp.where(row >= base + PANEL, lower, work)
        for step in range(PANEL):
            work = jnp.where(row == base + step, leads[step], work)
    return work


def lanes(matrix, place):
    return (pltpu.roll(matrix, 128 - K * place, 1) if place else matrix)[:, :K]


def upper_part(matrix):
    return jnp.where(iota((K, K), 1) >= iota((K, K), 0), matrix, 0.0)


def flip(matrix):
    eye = jnp.where(iota((K, K), 0) == iota((K, K), 1), 1.0, 0.0)
    return dot_t(eye, matrix)


def fill(message, rows):
    for device in range(message.shape[0]):
        message[device, : rows.shape[0], :] = rows


def stage_kernel(tiles, staged, turned):
    for tile in range(tiles.shape[0]):
        staged[tile] = tiles[tile]
        turned[tile] = tiles[tile].T


def prepare_kernel(start, message):
    fill(message, start[...].astype(bf16))


def pack(square, cross):
    row, column = iota((K, 128), 0), iota((K, 128), 1)
    both = jnp.where(column < K, jnp.where(row >= column, square, cross), 0.0)
    quarter = K // 4
    folded = both[:quarter]
    for place in range(1, 4):
        folded += pltpu.roll(both[place * quarter : (place + 1) * quarter], K * place, 1)
    middle = jnp.sum(jnp.where(row == column, cross, 0.0), axis=0, keepdims=True)
    return jnp.concatenate([folded[line : line + 1] for line in range(quarter)] + [middle], axis=1)


def unpack(packed):
    quarter = K // 4
    folded = jnp.concatenate([packed[:, 128 * line : 128 * (line + 1)] for line in range(quarter)])
    both = jnp.concatenate([lanes(folded, place) for place in range(4)])
    other = flip(both)
    row, column = iota((K, K), 0), iota((K, K), 1)
    square = jnp.where(row >= column, both, other)
    middle = packed[:, 128 * quarter : 128 * quarter + K]
    cross = jnp.where(row < column, both, jnp.where(row == column, middle, other))
    return square, cross


def lower_kernel(lists, got, tiles, message, total):
    total[...] = jnp.zeros_like(total)
    count = tiles.shape[0]
    for base in range(0, count, GROUP):
        parts = []
        for tile in range(base, base + GROUP):
            place = lists[tile]
            vectors = got[place >> 1, pl.ds(pl.multiple_of((place & 1) * K, K), K), :]
            parts.append(jnp.dot(vectors, tiles[tile], preferred_element_type=f32))
        for tile in range(base, base + GROUP):
            place = lists[count + tile]
            owner = place >> 1
            near = (owner >> 4) * 2 + (owner & 1)
            spot = (near * FARS + ((owner >> 1) & 7)) * 2 + (place & 1)
            where = pl.ds(pl.multiple_of(spot * K, K), K)
            total[where, :] += parts[tile - base]
    message[:, :SLAB, :] = total[...].astype(bf16).reshape(NEARS, SLAB, 128)
    if got.shape[1] > OWN:
        piece = sum_slices(got[:, OWN:, :].reshape(COLUMNS * EXTRA, 128))
        for device in range(NEARS):
            message[device, SLAB:, :] = piece


def near_kernel(got, vectors, message):
    total = got[0, :SLAB, :].astype(f32)
    for device in range(1, NEARS):
        total += got[device, :SLAB, :].astype(f32)
    message[:, OWN : 2 * OWN, :] = total.astype(bf16).reshape(FARS, OWN, 128)
    fill(message, vectors[...].astype(bf16))
    if got.shape[1] > SLAB:
        piece = sum_slices(got[:, SLAB:, :].reshape(NEARS * EXTRA, 128))
        for device in range(FARS):
            message[device, 2 * OWN :, :] = piece


def far_kernel(got, message, column_sums, *piece):
    total = got[0, OWN : 2 * OWN, :].astype(f32)
    for device in range(1, FARS):
        total += got[device, OWN : 2 * OWN, :].astype(f32)
    column_sums[...] = total
    if piece:
        piece[0][...] = sum_slices(got[:, 2 * OWN :, :].reshape(FARS * EXTRA, 128))
    fill(message, got[:, :OWN, :].reshape(SLAB, 128))


def upper_kernel(lists, got, tiles, *refs):
    *piece, message, total = refs
    total[...] = jnp.zeros_like(total)
    count = tiles.shape[0]
    for base in range(0, count, GROUP):
        parts = []
        for tile in range(base, base + GROUP):
            place = lists[count + tile]
            owner = place >> 1
            near = (owner >> 4) * 2 + (owner & 1)
            spot = ((owner >> 1) & 7) * 2 + (place & 1)
            vectors = got[near, pl.ds(pl.multiple_of(spot * K, K), K), :]
            parts.append(jnp.dot(vectors, tiles[tile], preferred_element_type=f32))
        for tile in range(base, base + GROUP):
            where = pl.ds(pl.multiple_of(lists[tile] * K, K), K)
            total[where, :] += parts[tile - base]
    message[:, :OWN, :] = total[...].astype(bf16).reshape(COLUMNS, OWN, 128)
    if piece:
        for device in range(COLUMNS):
            message[device, OWN:, :] = piece[0][...]


def image_of(got, column_sums, vectors, diagonal):
    images = []
    for block in range(OWN // K):
        where = slice(block * K, (block + 1) * K)
        narrow = vectors[where, :].astype(bf16)
        image = dot_t(narrow, diagonal[block], None)
        image += jnp.dot(narrow, diagonal[block], preferred_element_type=f32)
        image = 0.5 * image + column_sums[where, :]
        total = got[0, where, :].astype(f32)
        for device in range(1, COLUMNS):
            total += got[device, where, :].astype(f32)
        images.append(image + total)
    return images


def middle_kernel(got, column_sums, start, diagonal, image, message):
    images = image_of(got, column_sums, start, diagonal)
    grams = jnp.zeros((K, 128), f32)
    empty = jnp.zeros((K, 128), f32)
    for block in range(OWN // K):
        where = slice(block * K, (block + 1) * K)
        vectors = start[where, :]
        image[where, :] = images[block]
        pair = [vectors, images[block]]
        grams += dot_t(vectors, jnp.concatenate(pair + [empty, empty]))
        grams += dot_t(images[block], jnp.concatenate([empty, empty] + pair))
    fill(message, jnp.concatenate(images).astype(bf16))
    message[:, OWN:, :] = spread_slices(grams).reshape(COLUMNS, EXTRA, 128)


def finish_kernel(
    got, column_sums, start, first, diagonal, basis, image, alpha, beta, message
):
    images = image_of(got, column_sums, first, diagonal)
    sums = join_slices(got[:, OWN:, :].reshape(COLUMNS * EXTRA, 128))
    work = eliminate(jnp.concatenate([sums, pltpu.roll(sums, 128 - 2 * K, 1)]))
    upper = upper_part(lanes(work[K:], 1))
    inverse = lanes(work[:K], 2)
    weights = pltpu.roll(work[K:], 128 - 2 * K, 1)[:, : 2 * K]
    back = dot(dot_t(upper, inverse), inverse)
    square = jnp.zeros((K, 128), f32)
    cross = jnp.zeros((K, 128), f32)
    empty = [jnp.zeros((K, 128), f32)] * 3
    for block in range(OWN // K):
        where = slice(block * K, (block + 1) * K)
        current = dot(weights, jnp.concatenate([start[where, :], first[where, :]]))
        result = dot(weights, jnp.concatenate([first[where, :], images[block]]))
        result -= dot(back, start[where, :])
        basis[where, :] = current
        image[where, :] = result
        wide = jnp.concatenate([result] + empty)
        square += dot_t(result, wide)
        cross += dot_t(current, wide)
    packed = pack(square, cross)
    for device in range(message.shape[0]):
        message[device] = packed
    alpha[...] = dot_t(lanes(work[:K], 1), inverse)
    beta[...] = dot_t(inverse, upper)


def plane_kernel(got, message):
    total = got[0]
    for device in range(1, got.shape[0]):
        total += got[device]
    for device in range(message.shape[0]):
        message[device, :, :] = total


def last_kernel(scaling, got, basis, image, alpha_first, beta_first, result, alphas, betas):
    total = got[0]
    for device in range(1, got.shape[0]):
        total += got[device]
    image_gram, alpha_last = unpack(total)
    wide = jnp.zeros((K, 128 - K), f32)
    work = eliminate(jnp.concatenate([image_gram - dot(alpha_last, alpha_last), wide], axis=1))
    upper, inverse = upper_part(work[:, :K]), lanes(work, 1)
    for block in range(OWN // K):
        where = slice(block * K, (block + 1) * K)
        residual = image[where, :] - dot(alpha_last, basis[where, :])
        result[where, :] = dot(inverse, residual) * scaling
    alphas[0] = alpha_first[...]
    alphas[1] = alpha_last
    betas[0] = beta_first[...]
    betas[1] = flip(upper)


def exchange(message, vectors, tiles, turned, lists):
    extra = message.shape[1] - OWN
    got = swap(message, COLUMN)
    sent = call(
        lower_kernel,
        out((NEARS, SLAB + extra, 128), bf16),
        (lists,),
        (got, tiles),
        (pltpu.VMEM((NEARS * SLAB, 128), f32),),
    )
    got = swap(sent, NEAR)
    sent = call(near_kernel, out((FARS, 2 * OWN + extra, 128), bf16), (), (got, vectors))
    got = swap(sent, FAR)
    outs = [out((NEARS, SLAB, 128), bf16), out((OWN, 128), f32)]
    if extra:
        outs.append(out((extra, 128), bf16))
    sent, column_sums, *piece = call(far_kernel, outs, (), (got,))
    got = swap(sent, NEAR)
    sent = call(
        upper_kernel,
        out((COLUMNS, OWN + extra, 128), bf16),
        (lists,),
        (got, turned, *piece),
        (pltpu.VMEM((COLUMNS * OWN, 128), f32),),
    )
    return swap(sent, COLUMN), column_sums


def local(start_block, tile_values, tile_rows, tile_columns, diagonal_blocks):
    start = start_block.reshape(OWN, 128)
    tiles = tile_values[0, 0]
    matrix = (
        *call(stage_kernel, (out(tiles.shape, bf16), out(tiles.shape, bf16)), (), (tiles,)),
        jnp.concatenate([tile_rows[0, 0], tile_columns[0, 0]]),
    )
    vectors = out((OWN, 128), f32)
    square = out((K, K), f32)
    message = call(prepare_kernel, out((COLUMNS, OWN, 128), bf16), (), (start,))
    got, column_sums = exchange(message, start, *matrix)
    first, message = call(
        middle_kernel,
        (vectors, out((COLUMNS, OWN + EXTRA, 128), bf16)),
        (),
        (got, column_sums, start, diagonal_blocks),
    )
    got, column_sums = exchange(message, first, *matrix)
    planes, depths = lax.axis_size(PLANE), lax.axis_size(DEPTH)
    basis, image, alpha_first, beta_first, message = call(
        finish_kernel,
        (vectors, vectors, square, square, out((planes, 1, PACKED), f32)),
        (),
        (got, column_sums, start, first, diagonal_blocks),
    )
    got = swap(message, PLANE)
    message = call(plane_kernel, out((depths, 1, PACKED), f32), (), (got,))
    got = swap(message, DEPTH)
    scaling = math.sqrt(start_block.shape[0] * start_block.shape[2] * planes * depths)
    pair = out((2, K, K), f32)
    result, alphas, betas = call(
        functools.partial(last_kernel, scaling),
        (vectors, pair, pair),
        (),
        (got, basis, image, alpha_first, beta_first),
    )
    return result.reshape(start_block.shape), alphas, betas


def solution(mesh):
    split = Mesh(mesh.devices.reshape(2, FARS, 2, 2, 4, 2), AXES)
    rows = ("x_high", "far", "near")
    owner = P((*COLUMN, *rows), None, None)
    placed = (
        owner,
        P(rows, COLUMN, None, None, None),
        P(rows, COLUMN, None),
        P(rows, COLUMN, None),
        owner,
    )
    return jax.shard_map(
        local,
        mesh=split,
        in_specs=placed,
        out_specs=(owner, P(), P()),
        check_vma=False,
    )
```

```python
import functools
import math

import jax
import jax.numpy as jnp
from jax import lax
from jax.experimental import pallas as pl
from jax.experimental.pallas import tpu as pltpu
from jax.sharding import Mesh
from jax.sharding import PartitionSpec as P

AXES = ("x_high", "far", "near", "x_low", "y", "core")
COLUMN = ("x_low", "y", "core")
PLANE = ("x_high", *COLUMN)
DEPTH = ("far", "near")
NEAR = ("x_high", "near")
FAR = ("far",)

NEARS = 4
FARS = 8
COLUMNS = 16
K = 32
OWN = 64
SLAB = FARS * OWN
EXTRA = 16
TERMS = 3
GROUP = 8
PANEL = 16
PACKED = K * K + 128

highest = lax.Precision.HIGHEST
f32 = jnp.float32
bf16 = jnp.bfloat16


def swap(parts, axis):
    return lax.all_to_all(parts, axis, 0, 0, tiled=True)


def call(kernel, outs, scalars, arrays, scratch=()):
    specs = [pl.BlockSpec(memory_space=pltpu.SMEM)] * len(scalars)
    specs += [pl.BlockSpec(memory_space=pltpu.VMEM)] * len(arrays)
    return pl.pallas_call(
        kernel,
        out_shape=outs,
        in_specs=specs,
        out_specs=jax.tree.map(lambda _: pl.BlockSpec(memory_space=pltpu.VMEM), outs),
        scratch_shapes=list(scratch),
        compiler_params=pltpu.CompilerParams(vmem_limit_bytes=16 * 2**20),
    )(*scalars, *arrays)


def out(shape, dtype):
    return jax.ShapeDtypeStruct(shape, dtype)


def iota(shape, dimension):
    return lax.broadcasted_iota(jnp.int32, shape, dimension)


def dot(left, right):
    return jnp.dot(left, right, precision=highest, preferred_element_type=f32)


def dot_t(left, right, precision=highest):
    return lax.dot_general(
        left, right, (((1,), (1,)), ((), ())), precision=precision, preferred_element_type=f32
    )


def terms_of(values):
    high = values.astype(bf16)
    rest = values - high.astype(f32)
    middle = rest.astype(bf16)
    low = (rest - middle.astype(f32)).astype(bf16)
    return high, middle, low


def one_hot(condition):
    return jnp.where(condition, 1.0, 0.0).astype(bf16)


def spread_slices(grams):
    source = jnp.concatenate(terms_of(grams), axis=0)
    shape = (COLUMNS * EXTRA, TERMS * K)
    row, column = iota(shape, 0), iota(shape, 1)
    place = row & (EXTRA - 1)
    wanted = (place >> 1) * K + (row >> 4) * 2 + (place & 1)
    picker = one_hot((place < 2 * TERMS) & (column == wanted))
    return jnp.dot(picker, source, preferred_element_type=f32).astype(bf16)


def sum_slices(pieces):
    shape = (EXTRA, pieces.shape[0])
    row, column = iota(shape, 0), iota(shape, 1)
    picker = one_hot(((column & 15) < 2 * TERMS) & ((column & 1) == (row & 1)))
    total = jnp.dot(picker, pieces, preferred_element_type=f32)
    high, middle, low = (term.astype(f32) for term in terms_of(total))
    place = iota(total.shape, 0)
    chosen = jnp.where(place < 2, high, jnp.where(place < 4, middle, low))
    return jnp.where(place < 2 * TERMS, chosen, 0.0).astype(bf16)


def join_slices(pieces):
    shape = (K, pieces.shape[0])
    row, column = iota(shape, 0), iota(shape, 1)
    picker = one_hot(
        ((column >> 4) == (row >> 1)) & ((column & 15) < 2 * TERMS) & ((column & 1) == (row & 1))
    )
    return jnp.dot(picker, pieces, preferred_element_type=f32)


def eliminate(gram):
    count = gram.shape[0]
    shape = (count, 128)
    row, column = iota(shape, 0), iota(shape, 1)
    work = jnp.where(column < count, gram, jnp.where(column == row + count, 1.0, 0.0))
    for base in range(0, count, PANEL):
        columns = [
            jnp.broadcast_to(work[:, base + step : base + step + 1], shape) for step in range(PANEL)
        ]
        leads = [work[base + step : base + step + 1, :] for step in range(PANEL)]
        for step in range(PANEL):
            scale = lax.rsqrt(columns[step][base + step : base + step + 1, :])
            columns[step] *= scale
            leads[step] *= scale
            for later in range(step + 1, PANEL):
                share = columns[step][base + later : base + later + 1, :]
                columns[later] -= columns[step] * share
                leads[later] -= leads[step] * share
        lower = work
        for step in range(PANEL):
            lower -= columns[step] * leads[step]
        work = jnp.where(row >= base + PANEL, lower, work)
        for step in range(PANEL):
            work = jnp.where(row == base + step, leads[step], work)
    return work


def lanes(matrix, place):
    return (pltpu.roll(matrix, 128 - K * place, 1) if place else matrix)[:, :K]


def upper_part(matrix):
    return jnp.where(iota((K, K), 1) >= iota((K, K), 0), matrix, 0.0)


def fill(message, rows):
    for device in range(message.shape[0]):
        message[device, : rows.shape[0], :] = rows


def stage_kernel(tiles, staged, turned):
    for tile in range(tiles.shape[0]):
        staged[tile] = tiles[tile]
        turned[tile] = tiles[tile].T


def prepare_kernel(start, message):
    fill(message, start[...].astype(bf16))


def pack(square, cross):
    row, column = iota((K, 128), 0), iota((K, 128), 1)
    both = jnp.where(column < K, jnp.where(row >= column, square, cross), 0.0)
    quarter = K // 4
    folded = both[:quarter]
    for place in range(1, 4):
        folded += pltpu.roll(both[place * quarter : (place + 1) * quarter], K * place, 1)
    middle = jnp.sum(jnp.where(row == column, cross, 0.0), axis=0, keepdims=True)
    return jnp.concatenate([folded[line : line + 1] for line in range(quarter)] + [middle], axis=1)


def unpack(packed):
    quarter = K // 4
    folded = jnp.concatenate([packed[:, 128 * line : 128 * (line + 1)] for line in range(quarter)])
    both = jnp.concatenate([lanes(folded, place) for place in range(4)])
    other = both.T
    row, column = iota((K, K), 0), iota((K, K), 1)
    square = jnp.where(row >= column, both, other)
    middle = packed[:, 128 * quarter : 128 * quarter + K]
    cross = jnp.where(row < column, both, jnp.where(row == column, middle, other))
    return square, cross


def lower_kernel(lists, got, tiles, message, total):
    total[...] = jnp.zeros_like(total)
    count = tiles.shape[0]
    for base in range(0, count, GROUP):
        parts = []
        for tile in range(base, base + GROUP):
            place = lists[tile]
            vectors = got[place >> 1, pl.ds(pl.multiple_of((place & 1) * K, K), K), :]
            parts.append(jnp.dot(vectors, tiles[tile], preferred_element_type=f32))
        for tile in range(base, base + GROUP):
            place = lists[count + tile]
            owner = place >> 1
            near = (owner >> 4) * 2 + (owner & 1)
            spot = (near * FARS + ((owner >> 1) & 7)) * 2 + (place & 1)
            where = pl.ds(pl.multiple_of(spot * K, K), K)
            total[where, :] += parts[tile - base]
    message[:, :SLAB, :] = total[...].astype(bf16).reshape(NEARS, SLAB, 128)
    if got.shape[1] > OWN:
        piece = sum_slices(got[:, OWN:, :].reshape(COLUMNS * EXTRA, 128))
        for device in range(NEARS):
            message[device, SLAB:, :] = piece


def near_kernel(got, vectors, message):
    total = got[0, :SLAB, :].astype(f32)
    for device in range(1, NEARS):
        total += got[device, :SLAB, :].astype(f32)
    message[:, OWN : 2 * OWN, :] = total.astype(bf16).reshape(FARS, OWN, 128)
    fill(message, vectors[...].astype(bf16))
    if got.shape[1] > SLAB:
        piece = sum_slices(got[:, SLAB:, :].reshape(NEARS * EXTRA, 128))
        for device in range(FARS):
            message[device, 2 * OWN :, :] = piece


def far_kernel(got, message, column_sums, *piece):
    total = got[0, OWN : 2 * OWN, :].astype(f32)
    for device in range(1, FARS):
        total += got[device, OWN : 2 * OWN, :].astype(f32)
    column_sums[...] = total
    if piece:
        piece[0][...] = sum_slices(got[:, 2 * OWN :, :].reshape(FARS * EXTRA, 128))
    fill(message, got[:, :OWN, :].reshape(SLAB, 128))


def upper_kernel(lists, got, tiles, *refs):
    *piece, message, total = refs
    total[...] = jnp.zeros_like(total)
    count = tiles.shape[0]
    for base in range(0, count, GROUP):
        parts = []
        for tile in range(base, base + GROUP):
            place = lists[count + tile]
            owner = place >> 1
            near = (owner >> 4) * 2 + (owner & 1)
            spot = ((owner >> 1) & 7) * 2 + (place & 1)
            vectors = got[near, pl.ds(pl.multiple_of(spot * K, K), K), :]
            parts.append(jnp.dot(vectors, tiles[tile], preferred_element_type=f32))
        for tile in range(base, base + GROUP):
            where = pl.ds(pl.multiple_of(lists[tile] * K, K), K)
            total[where, :] += parts[tile - base]
    message[:, :OWN, :] = total[...].astype(bf16).reshape(COLUMNS, OWN, 128)
    if piece:
        for device in range(COLUMNS):
            message[device, OWN:, :] = piece[0][...]


def image_of(got, column_sums, vectors, diagonal):
    images = []
    for block in range(OWN // K):
        where = slice(block * K, (block + 1) * K)
        narrow = vectors[where, :].astype(bf16)
        image = dot_t(narrow, diagonal[block], None)
        image += jnp.dot(narrow, diagonal[block], preferred_element_type=f32)
        image = 0.5 * image + column_sums[where, :]
        total = got[0, where, :].astype(f32)
        for device in range(1, COLUMNS):
            total += got[device, where, :].astype(f32)
        images.append(image + total)
    return images


def middle_kernel(got, column_sums, start, diagonal, image, message):
    images = image_of(got, column_sums, start, diagonal)
    grams = jnp.zeros((K, 128), f32)
    empty = jnp.zeros((K, 128), f32)
    for block in range(OWN // K):
        where = slice(block * K, (block + 1) * K)
        vectors = start[where, :]
        image[where, :] = images[block]
        pair = [vectors, images[block]]
        grams += dot_t(vectors, jnp.concatenate(pair + [empty, empty]))
        grams += dot_t(images[block], jnp.concatenate([empty, empty] + pair))
    fill(message, jnp.concatenate(images).astype(bf16))
    message[:, OWN:, :] = spread_slices(grams).reshape(COLUMNS, EXTRA, 128)


def finish_kernel(
    got, column_sums, start, first, diagonal, basis, image, alpha, beta, message
):
    images = image_of(got, column_sums, first, diagonal)
    sums = join_slices(got[:, OWN:, :].reshape(COLUMNS * EXTRA, 128))
    work = eliminate(jnp.concatenate([sums, pltpu.roll(sums, 128 - 2 * K, 1)]))
    upper = upper_part(lanes(work[K:], 1))
    inverse = lanes(work[:K], 2)
    weights = pltpu.roll(work[K:], 128 - 2 * K, 1)[:, : 2 * K]
    back = dot(dot_t(upper, inverse), inverse)
    square = jnp.zeros((K, 128), f32)
    cross = jnp.zeros((K, 128), f32)
    empty = [jnp.zeros((K, 128), f32)] * 3
    for block in range(OWN // K):
        where = slice(block * K, (block + 1) * K)
        current = dot(weights, jnp.concatenate([start[where, :], first[where, :]]))
        result = dot(weights, jnp.concatenate([first[where, :], images[block]]))
        result -= dot(back, start[where, :])
        basis[where, :] = current
        image[where, :] = result
        wide = jnp.concatenate([result] + empty)
        square += dot_t(result, wide)
        cross += dot_t(current, wide)
    packed = pack(square, cross)
    for device in range(message.shape[0]):
        message[device] = packed
    alpha[...] = dot_t(lanes(work[:K], 1), inverse)
    beta[...] = dot_t(inverse, upper)


def plane_kernel(got, message):
    total = got[0]
    for device in range(1, got.shape[0]):
        total += got[device]
    for device in range(message.shape[0]):
        message[device, :, :] = total


def last_kernel(scaling, got, basis, image, alpha_first, beta_first, result, alphas, betas):
    total = got[0]
    for device in range(1, got.shape[0]):
        total += got[device]
    image_gram, alpha_last = unpack(total)
    wide = jnp.zeros((K, 128 - K), f32)
    work = eliminate(jnp.concatenate([image_gram - dot(alpha_last, alpha_last), wide], axis=1))
    upper, inverse = upper_part(work[:, :K]), lanes(work, 1)
    for block in range(OWN // K):
        where = slice(block * K, (block + 1) * K)
        residual = image[where, :] - dot(alpha_last, basis[where, :])
        result[where, :] = dot(inverse, residual) * scaling
    alphas[0] = alpha_first[...]
    alphas[1] = alpha_last
    betas[0] = beta_first[...]
    betas[1] = upper.T


def exchange(message, vectors, tiles, turned, lists):
    extra = message.shape[1] - OWN
    got = swap(message, COLUMN)
    sent = call(
        lower_kernel,
        out((NEARS, SLAB + extra, 128), bf16),
        (lists,),
        (got, tiles),
        (pltpu.VMEM((NEARS * SLAB, 128), f32),),
    )
    got = swap(sent, NEAR)
    sent = call(near_kernel, out((FARS, 2 * OWN + extra, 128), bf16), (), (got, vectors))
    got = swap(sent, FAR)
    outs = [out((NEARS, SLAB, 128), bf16), out((OWN, 128), f32)]
    if extra:
        outs.append(out((extra, 128), bf16))
    sent, column_sums, *piece = call(far_kernel, outs, (), (got,))
    got = swap(sent, NEAR)
    sent = call(
        upper_kernel,
        out((COLUMNS, OWN + extra, 128), bf16),
        (lists,),
        (got, turned, *piece),
        (pltpu.VMEM((COLUMNS * OWN, 128), f32),),
    )
    return swap(sent, COLUMN), column_sums


def local(start_block, tile_values, tile_rows, tile_columns, diagonal_blocks):
    start = start_block.reshape(OWN, 128)
    tiles = tile_values[0, 0]
    matrix = (
        *call(stage_kernel, (out(tiles.shape, bf16), out(tiles.shape, bf16)), (), (tiles,)),
        jnp.concatenate([tile_rows[0, 0], tile_columns[0, 0]]),
    )
    vectors = out((OWN, 128), f32)
    square = out((K, K), f32)
    message = call(prepare_kernel, out((COLUMNS, OWN, 128), bf16), (), (start,))
    got, column_sums = exchange(message, start, *matrix)
    first, message = call(
        middle_kernel,
        (vectors, out((COLUMNS, OWN + EXTRA, 128), bf16)),
        (),
        (got, column_sums, start, diagonal_blocks),
    )
    got, column_sums = exchange(message, first, *matrix)
    planes, depths = lax.axis_size(PLANE), lax.axis_size(DEPTH)
    basis, image, alpha_first, beta_first, message = call(
        finish_kernel,
        (vectors, vectors, square, square, out((planes, 1, PACKED), f32)),
        (),
        (got, column_sums, start, first, diagonal_blocks),
    )
    got = swap(message, PLANE)
    message = call(plane_kernel, out((depths, 1, PACKED), f32), (), (got,))
    got = swap(message, DEPTH)
    scaling = math.sqrt(start_block.shape[0] * start_block.shape[2] * planes * depths)
    pair = out((2, K, K), f32)
    result, alphas, betas = call(
        functools.partial(last_kernel, scaling),
        (vectors, pair, pair),
        (),
        (got, basis, image, alpha_first, beta_first),
    )
    return result.reshape(start_block.shape), alphas, betas


def solution(mesh):
    split = Mesh(mesh.devices.reshape(2, FARS, 2, 2, 4, 2), AXES)
    rows = ("x_high", "far", "near")
    owner = P((*COLUMN, *rows), None, None)
    placed = (
        owner,
        P(rows, COLUMN, None, None, None),
        P(rows, COLUMN, None),
        P(rows, COLUMN, None),
        owner,
    )
    return jax.shard_map(
        local,
        mesh=split,
        in_specs=placed,
        out_specs=(owner, P(), P()),
        check_vma=False,
    )
```

```python
import functools
import math

import jax
import jax.numpy as jnp
from jax import lax
from jax.experimental import pallas as pl
from jax.experimental.pallas import tpu as pltpu
from jax.sharding import Mesh
from jax.sharding import PartitionSpec as P

AXES = ("x_high", "far", "near", "x_low", "y", "core")
COLUMN = ("x_low", "y", "core")
PLANE = ("x_high", *COLUMN)
DEPTH = ("far", "near")
NEAR = ("x_high", "near")
FAR = ("far",)

NEARS = 4
FARS = 8
COLUMNS = 16
K = 32
OWN = 64
SLAB = FARS * OWN
EXTRA = 16
TERMS = 3
GROUP = 8
PANEL = 16
PACKED = K * K + 128

highest = lax.Precision.HIGHEST
f32 = jnp.float32
bf16 = jnp.bfloat16


def swap(parts, axis):
    return lax.all_to_all(parts, axis, 0, 0, tiled=True)


def call(kernel, outs, scalars, arrays, scratch=()):
    specs = [pl.BlockSpec(memory_space=pltpu.SMEM)] * len(scalars)
    specs += [pl.BlockSpec(memory_space=pltpu.VMEM)] * len(arrays)
    return pl.pallas_call(
        kernel,
        out_shape=outs,
        in_specs=specs,
        out_specs=jax.tree.map(lambda _: pl.BlockSpec(memory_space=pltpu.VMEM), outs),
        scratch_shapes=list(scratch),
        compiler_params=pltpu.CompilerParams(vmem_limit_bytes=16 * 2**20),
    )(*scalars, *arrays)


def out(shape, dtype):
    return jax.ShapeDtypeStruct(shape, dtype)


def iota(shape, dimension):
    return lax.broadcasted_iota(jnp.int32, shape, dimension)


def dot(left, right):
    return jnp.dot(left, right, precision=highest, preferred_element_type=f32)


def dot_t(left, right, precision=highest):
    return lax.dot_general(
        left, right, (((1,), (1,)), ((), ())), precision=precision, preferred_element_type=f32
    )


def terms_of(values):
    high = values.astype(bf16)
    rest = values - high.astype(f32)
    middle = rest.astype(bf16)
    low = (rest - middle.astype(f32)).astype(bf16)
    return high, middle, low


def one_hot(condition):
    return jnp.where(condition, 1.0, 0.0).astype(bf16)


def spread_slices(grams):
    source = jnp.concatenate(terms_of(grams), axis=0)
    shape = (COLUMNS * EXTRA, TERMS * K)
    row, column = iota(shape, 0), iota(shape, 1)
    place = row & (EXTRA - 1)
    wanted = (place >> 1) * K + (row >> 4) * 2 + (place & 1)
    picker = one_hot((place < 2 * TERMS) & (column == wanted))
    return jnp.dot(picker, source, preferred_element_type=f32).astype(bf16)


def sum_slices(pieces):
    shape = (EXTRA, pieces.shape[0])
    row, column = iota(shape, 0), iota(shape, 1)
    picker = one_hot(((column & 15) < 2 * TERMS) & ((column & 1) == (row & 1)))
    total = jnp.dot(picker, pieces, preferred_element_type=f32)
    high, middle, low = (term.astype(f32) for term in terms_of(total))
    place = iota(total.shape, 0)
    chosen = jnp.where(place < 2, high, jnp.where(place < 4, middle, low))
    return jnp.where(place < 2 * TERMS, chosen, 0.0).astype(bf16)


def join_slices(pieces):
    shape = (K, pieces.shape[0])
    row, column = iota(shape, 0), iota(shape, 1)
    picker = one_hot(
        ((column >> 4) == (row >> 1)) & ((column & 15) < 2 * TERMS) & ((column & 1) == (row & 1))
    )
    return jnp.dot(picker, pieces, preferred_element_type=f32)


def eliminate(gram):
    count = gram.shape[0]
    shape = (count, 128)
    row, column = iota(shape, 0), iota(shape, 1)
    work = jnp.where(column < count, gram, jnp.where(column == row + count, 1.0, 0.0))
    for base in range(0, count, PANEL):
        columns = [
            jnp.broadcast_to(work[:, base + step : base + step + 1], shape) for step in range(PANEL)
        ]
        leads = [work[base + step : base + step + 1, :] for step in range(PANEL)]
        for step in range(PANEL):
            scale = lax.rsqrt(columns[step][base + step : base + step + 1, :])
            columns[step] *= scale
            leads[step] *= scale
            for later in range(step + 1, PANEL):
                share = columns[step][base + later : base + later + 1, :]
                columns[later] -= columns[step] * share
                leads[later] -= leads[step] * share
        lower = work
        for step in range(PANEL):
            lower -= columns[step] * leads[step]
        work = jnp.where(row >= base + PANEL, lower, work)
        for step in range(PANEL):
            work = jnp.where(row == base + step, leads[step], work)
    return work


def lanes(matrix, place):
    return (pltpu.roll(matrix, 128 - K * place, 1) if place else matrix)[:, :K]


def upper_part(matrix):
    return jnp.where(iota((K, K), 1) >= iota((K, K), 0), matrix, 0.0)


def fill(message, rows):
    for device in range(message.shape[0]):
        message[device, : rows.shape[0], :] = rows


def stage_kernel(tiles, staged, turned):
    for tile in range(tiles.shape[0]):
        staged[tile] = tiles[tile]
        turned[tile] = tiles[tile].T


def prepare_kernel(start, message):
    fill(message, start[...].astype(bf16))


def pack(square, cross):
    row, column = iota((K, K), 0), iota((K, K), 1)
    wide = jnp.zeros((K, 128 - K), f32)
    both = jnp.concatenate([jnp.where(row >= column, square, cross), wide], axis=1)
    quarter = K // 4
    folded = both[:quarter]
    for place in range(1, 4):
        folded += pltpu.roll(both[place * quarter : (place + 1) * quarter], K * place, 1)
    middle = jnp.concatenate([jnp.where(row == column, cross, 0.0), wide], axis=1)
    middle = jnp.sum(middle, axis=0, keepdims=True)
    return jnp.concatenate([folded[line : line + 1] for line in range(quarter)] + [middle], axis=1)


def unpack(packed):
    quarter = K // 4
    folded = jnp.concatenate([packed[:, 128 * line : 128 * (line + 1)] for line in range(quarter)])
    both = jnp.concatenate([lanes(folded, place) for place in range(4)])
    other = both.T
    row, column = iota((K, K), 0), iota((K, K), 1)
    square = jnp.where(row >= column, both, other)
    middle = packed[:, 128 * quarter : 128 * quarter + K]
    cross = jnp.where(row < column, both, jnp.where(row == column, middle, other))
    return square, cross


def lower_kernel(lists, got, tiles, message, total):
    total[...] = jnp.zeros_like(total)
    count = tiles.shape[0]
    for base in range(0, count, GROUP):
        parts = []
        for tile in range(base, base + GROUP):
            place = lists[tile]
            vectors = got[place >> 1, pl.ds(pl.multiple_of((place & 1) * K, K), K), :]
            parts.append(jnp.dot(vectors, tiles[tile], preferred_element_type=f32))
        for tile in range(base, base + GROUP):
            place = lists[count + tile]
            owner = place >> 1
            near = (owner >> 4) * 2 + (owner & 1)
            spot = (near * FARS + ((owner >> 1) & 7)) * 2 + (place & 1)
            where = pl.ds(pl.multiple_of(spot * K, K), K)
            total[where, :] += parts[tile - base]
    message[:, :SLAB, :] = total[...].astype(bf16).reshape(NEARS, SLAB, 128)
    if got.shape[1] > OWN:
        piece = sum_slices(got[:, OWN:, :].reshape(COLUMNS * EXTRA, 128))
        for device in range(NEARS):
            message[device, SLAB:, :] = piece


def near_kernel(got, vectors, message):
    total = got[0, :SLAB, :].astype(f32)
    for device in range(1, NEARS):
        total += got[device, :SLAB, :].astype(f32)
    message[:, OWN : 2 * OWN, :] = total.astype(bf16).reshape(FARS, OWN, 128)
    fill(message, vectors[...].astype(bf16))
    if got.shape[1] > SLAB:
        piece = sum_slices(got[:, SLAB:, :].reshape(NEARS * EXTRA, 128))
        for device in range(FARS):
            message[device, 2 * OWN :, :] = piece


def far_kernel(got, message, column_sums, *piece):
    total = got[0, OWN : 2 * OWN, :].astype(f32)
    for device in range(1, FARS):
        total += got[device, OWN : 2 * OWN, :].astype(f32)
    column_sums[...] = total
    if piece:
        piece[0][...] = sum_slices(got[:, 2 * OWN :, :].reshape(FARS * EXTRA, 128))
    fill(message, got[:, :OWN, :].reshape(SLAB, 128))


def upper_kernel(lists, got, tiles, *refs):
    *piece, message, total = refs
    total[...] = jnp.zeros_like(total)
    count = tiles.shape[0]
    for base in range(0, count, GROUP):
        parts = []
        for tile in range(base, base + GROUP):
            place = lists[count + tile]
            owner = place >> 1
            near = (owner >> 4) * 2 + (owner & 1)
            spot = ((owner >> 1) & 7) * 2 + (place & 1)
            vectors = got[near, pl.ds(pl.multiple_of(spot * K, K), K), :]
            parts.append(jnp.dot(vectors, tiles[tile], preferred_element_type=f32))
        for tile in range(base, base + GROUP):
            where = pl.ds(pl.multiple_of(lists[tile] * K, K), K)
            total[where, :] += parts[tile - base]
    message[:, :OWN, :] = total[...].astype(bf16).reshape(COLUMNS, OWN, 128)
    if piece:
        for device in range(COLUMNS):
            message[device, OWN:, :] = piece[0][...]


def image_of(got, column_sums, vectors, diagonal):
    images = []
    for block in range(OWN // K):
        where = slice(block * K, (block + 1) * K)
        narrow = vectors[where, :].astype(bf16)
        image = dot_t(narrow, diagonal[block], None)
        image += jnp.dot(narrow, diagonal[block], preferred_element_type=f32)
        image = 0.5 * image + column_sums[where, :]
        total = got[0, where, :].astype(f32)
        for device in range(1, COLUMNS):
            total += got[device, where, :].astype(f32)
        images.append(image + total)
    return images


def middle_kernel(got, column_sums, start, diagonal, image, message):
    images = image_of(got, column_sums, start, diagonal)
    upper = jnp.zeros((K, 2 * K), f32)
    lower = jnp.zeros((K, 2 * K), f32)
    for block in range(OWN // K):
        where = slice(block * K, (block + 1) * K)
        vectors = start[where, :]
        image[where, :] = images[block]
        pair = jnp.concatenate([vectors, images[block]])
        upper += dot_t(vectors, pair)
        lower += dot_t(images[block], pair)
    fill(message, jnp.concatenate(images).astype(bf16))
    grams = jnp.concatenate([upper, lower], axis=1)
    message[:, OWN:, :] = spread_slices(grams).reshape(COLUMNS, EXTRA, 128)


def finish_kernel(
    got, column_sums, start, first, diagonal, basis, image, alpha, beta, message
):
    images = image_of(got, column_sums, first, diagonal)
    sums = join_slices(got[:, OWN:, :].reshape(COLUMNS * EXTRA, 128))
    work = eliminate(jnp.concatenate([sums, pltpu.roll(sums, 128 - 2 * K, 1)]))
    upper = upper_part(lanes(work[K:], 1))
    inverse = lanes(work[:K], 2)
    weights = pltpu.roll(work[K:], 128 - 2 * K, 1)[:, : 2 * K]
    back = dot(dot_t(upper, inverse), inverse)
    square = jnp.zeros((K, K), f32)
    cross = jnp.zeros((K, K), f32)
    for block in range(OWN // K):
        where = slice(block * K, (block + 1) * K)
        current = dot(weights, jnp.concatenate([start[where, :], first[where, :]]))
        result = dot(weights, jnp.concatenate([first[where, :], images[block]]))
        result -= dot(back, start[where, :])
        basis[where, :] = current
        image[where, :] = result
        square += dot_t(result, result)
        cross += dot_t(current, result)
    packed = pack(square, cross)
    for device in range(message.shape[0]):
        message[device] = packed
    alpha[...] = dot_t(lanes(work[:K], 1), inverse)
    beta[...] = dot_t(inverse, upper)


def plane_kernel(got, message):
    total = got[0]
    for device in range(1, got.shape[0]):
        total += got[device]
    for device in range(message.shape[0]):
        message[device, :, :] = total


def last_kernel(scaling, got, basis, image, alpha_first, beta_first, result, alphas, betas):
    total = got[0]
    for device in range(1, got.shape[0]):
        total += got[device]
    image_gram, alpha_last = unpack(total)
    wide = jnp.zeros((K, 128 - K), f32)
    work = eliminate(jnp.concatenate([image_gram - dot(alpha_last, alpha_last), wide], axis=1))
    upper, inverse = upper_part(work[:, :K]), lanes(work, 1)
    for block in range(OWN // K):
        where = slice(block * K, (block + 1) * K)
        residual = image[where, :] - dot(alpha_last, basis[where, :])
        result[where, :] = dot(inverse, residual) * scaling
    alphas[0] = alpha_first[...]
    alphas[1] = alpha_last
    betas[0] = beta_first[...]
    betas[1] = upper.T


def exchange(message, vectors, tiles, turned, lists):
    extra = message.shape[1] - OWN
    got = swap(message, COLUMN)
    sent = call(
        lower_kernel,
        out((NEARS, SLAB + extra, 128), bf16),
        (lists,),
        (got, tiles),
        (pltpu.VMEM((NEARS * SLAB, 128), f32),),
    )
    got = swap(sent, NEAR)
    sent = call(near_kernel, out((FARS, 2 * OWN + extra, 128), bf16), (), (got, vectors))
    got = swap(sent, FAR)
    outs = [out((NEARS, SLAB, 128), bf16), out((OWN, 128), f32)]
    if extra:
        outs.append(out((extra, 128), bf16))
    sent, column_sums, *piece = call(far_kernel, outs, (), (got,))
    got = swap(sent, NEAR)
    sent = call(
        upper_kernel,
        out((COLUMNS, OWN + extra, 128), bf16),
        (lists,),
        (got, turned, *piece),
        (pltpu.VMEM((COLUMNS * OWN, 128), f32),),
    )
    return swap(sent, COLUMN), column_sums


def local(start_block, tile_values, tile_rows, tile_columns, diagonal_blocks):
    start = start_block.reshape(OWN, 128)
    tiles = tile_values[0, 0]
    matrix = (
        *call(stage_kernel, (out(tiles.shape, bf16), out(tiles.shape, bf16)), (), (tiles,)),
        jnp.concatenate([tile_rows[0, 0], tile_columns[0, 0]]),
    )
    vectors = out((OWN, 128), f32)
    square = out((K, K), f32)
    message = call(prepare_kernel, out((COLUMNS, OWN, 128), bf16), (), (start,))
    got, column_sums = exchange(message, start, *matrix)
    first, message = call(
        middle_kernel,
        (vectors, out((COLUMNS, OWN + EXTRA, 128), bf16)),
        (),
        (got, column_sums, start, diagonal_blocks),
    )
    got, column_sums = exchange(message, first, *matrix)
    planes, depths = lax.axis_size(PLANE), lax.axis_size(DEPTH)
    basis, image, alpha_first, beta_first, message = call(
        finish_kernel,
        (vectors, vectors, square, square, out((planes, 1, PACKED), f32)),
        (),
        (got, column_sums, start, first, diagonal_blocks),
    )
    got = swap(message, PLANE)
    message = call(plane_kernel, out((depths, 1, PACKED), f32), (), (got,))
    got = swap(message, DEPTH)
    scaling = math.sqrt(start_block.shape[0] * start_block.shape[2] * planes * depths)
    pair = out((2, K, K), f32)
    result, alphas, betas = call(
        functools.partial(last_kernel, scaling),
        (vectors, pair, pair),
        (),
        (got, basis, image, alpha_first, beta_first),
    )
    return result.reshape(start_block.shape), alphas, betas


def solution(mesh):
    split = Mesh(mesh.devices.reshape(2, FARS, 2, 2, 4, 2), AXES)
    rows = ("x_high", "far", "near")
    owner = P((*COLUMN, *rows), None, None)
    placed = (
        owner,
        P(rows, COLUMN, None, None, None),
        P(rows, COLUMN, None),
        P(rows, COLUMN, None),
        owner,
    )
    return jax.shard_map(
        local,
        mesh=split,
        in_specs=placed,
        out_specs=(owner, P(), P()),
        check_vma=False,
    )
```

```python
import functools
import math

import jax
import jax.numpy as jnp
from jax import lax
from jax.experimental import pallas as pl
from jax.experimental.pallas import tpu as pltpu
from jax.sharding import Mesh
from jax.sharding import PartitionSpec as P

AXES = ("x_high", "far", "near", "x_low", "y", "core")
COLUMN = ("x_low", "y", "core")
PLANE = ("x_high", *COLUMN)
DEPTH = ("far", "near")
NEAR = ("x_high", "near")
FAR = ("far",)

NEARS = 4
FARS = 8
COLUMNS = 16
K = 32
OWN = 64
SLAB = FARS * OWN
EXTRA = 16
TERMS = 3
GROUP = 8
PANEL = 16
PACKED = K * K + 128

highest = lax.Precision.HIGHEST
f32 = jnp.float32
bf16 = jnp.bfloat16


def swap(parts, axis):
    return lax.all_to_all(parts, axis, 0, 0, tiled=True)


def call(kernel, outs, scalars, arrays, scratch=()):
    specs = [pl.BlockSpec(memory_space=pltpu.SMEM)] * len(scalars)
    specs += [pl.BlockSpec(memory_space=pltpu.VMEM)] * len(arrays)
    return pl.pallas_call(
        kernel,
        out_shape=outs,
        in_specs=specs,
        out_specs=jax.tree.map(lambda _: pl.BlockSpec(memory_space=pltpu.VMEM), outs),
        scratch_shapes=list(scratch),
        compiler_params=pltpu.CompilerParams(vmem_limit_bytes=16 * 2**20),
    )(*scalars, *arrays)


def out(shape, dtype):
    return jax.ShapeDtypeStruct(shape, dtype)


def iota(shape, dimension):
    return lax.broadcasted_iota(jnp.int32, shape, dimension)


def dot(left, right):
    return jnp.dot(left, right, precision=highest, preferred_element_type=f32)


def dot_t(left, right, precision=highest):
    return lax.dot_general(
        left, right, (((1,), (1,)), ((), ())), precision=precision, preferred_element_type=f32
    )


def terms_of(values):
    high = values.astype(bf16)
    rest = values - high.astype(f32)
    middle = rest.astype(bf16)
    low = (rest - middle.astype(f32)).astype(bf16)
    return high, middle, low


def one_hot(condition):
    return jnp.where(condition, 1.0, 0.0).astype(bf16)


def spread_slices(grams):
    source = jnp.concatenate(terms_of(grams), axis=0)
    shape = (COLUMNS * EXTRA, TERMS * K)
    row, column = iota(shape, 0), iota(shape, 1)
    place = row & (EXTRA - 1)
    wanted = (place >> 1) * K + (row >> 4) * 2 + (place & 1)
    picker = one_hot((place < 2 * TERMS) & (column == wanted))
    return jnp.dot(picker, source, preferred_element_type=f32).astype(bf16)


def sum_slices(pieces):
    shape = (EXTRA, pieces.shape[0])
    row, column = iota(shape, 0), iota(shape, 1)
    picker = one_hot(((column & 15) < 2 * TERMS) & ((column & 1) == (row & 1)))
    total = jnp.dot(picker, pieces, preferred_element_type=f32)
    high, middle, low = (term.astype(f32) for term in terms_of(total))
    place = iota(total.shape, 0)
    chosen = jnp.where(place < 2, high, jnp.where(place < 4, middle, low))
    return jnp.where(place < 2 * TERMS, chosen, 0.0).astype(bf16)


def join_slices(pieces):
    shape = (K, pieces.shape[0])
    row, column = iota(shape, 0), iota(shape, 1)
    picker = one_hot(
        ((column >> 4) == (row >> 1)) & ((column & 15) < 2 * TERMS) & ((column & 1) == (row & 1))
    )
    return jnp.dot(picker, pieces, preferred_element_type=f32)


def eliminate(gram):
    count = gram.shape[0]
    shape = (count, 128)
    row, column = iota(shape, 0), iota(shape, 1)
    work = jnp.where(column < count, gram, jnp.where(column == row + count, 1.0, 0.0))
    for base in range(0, count, PANEL):
        columns = [
            jnp.broadcast_to(work[:, base + step : base + step + 1], shape) for step in range(PANEL)
        ]
        leads = [work[base + step : base + step + 1, :] for step in range(PANEL)]
        for step in range(PANEL):
            scale = lax.rsqrt(columns[step][base + step : base + step + 1, :])
            columns[step] *= scale
            leads[step] *= scale
            for later in range(step + 1, PANEL):
                share = columns[step][base + later : base + later + 1, :]
                columns[later] -= columns[step] * share
                leads[later] -= leads[step] * share
        lower = work
        for step in range(PANEL):
            lower -= columns[step] * leads[step]
        work = jnp.where(row >= base + PANEL, lower, work)
        for step in range(PANEL):
            work = jnp.where(row == base + step, leads[step], work)
    return work


def lanes(matrix, place):
    return (pltpu.roll(matrix, 128 - K * place, 1) if place else matrix)[:, :K]


def upper_part(matrix):
    return jnp.where(iota((K, K), 1) >= iota((K, K), 0), matrix, 0.0)


def fill(message, rows):
    for device in range(message.shape[0]):
        message[device, : rows.shape[0], :] = rows


def stage_kernel(tiles, start, diagonal, staged, turned, part):
    for tile in range(tiles.shape[0]):
        staged[tile] = tiles[tile]
        turned[tile] = tiles[tile].T
    part[...] = jnp.concatenate(own_part(start, diagonal))


def prepare_kernel(start, message):
    fill(message, start[...].astype(bf16))


def pack(square, cross):
    row, column = iota((K, K), 0), iota((K, K), 1)
    wide = jnp.zeros((K, 128 - K), f32)
    both = jnp.concatenate([jnp.where(row >= column, square, cross), wide], axis=1)
    quarter = K // 4
    folded = both[:quarter]
    for place in range(1, 4):
        folded += pltpu.roll(both[place * quarter : (place + 1) * quarter], K * place, 1)
    middle = jnp.concatenate([jnp.where(row == column, cross, 0.0), wide], axis=1)
    middle = jnp.sum(middle, axis=0, keepdims=True)
    return jnp.concatenate([folded[line : line + 1] for line in range(quarter)] + [middle], axis=1)


def unpack(packed):
    quarter = K // 4
    folded = jnp.concatenate([packed[:, 128 * line : 128 * (line + 1)] for line in range(quarter)])
    both = jnp.concatenate([lanes(folded, place) for place in range(4)])
    other = both.T
    row, column = iota((K, K), 0), iota((K, K), 1)
    square = jnp.where(row >= column, both, other)
    middle = packed[:, 128 * quarter : 128 * quarter + K]
    cross = jnp.where(row < column, both, jnp.where(row == column, middle, other))
    return square, cross


def lower_kernel(lists, got, tiles, message, total):
    total[...] = jnp.zeros_like(total)
    count = tiles.shape[0]
    for base in range(0, count, GROUP):
        parts = []
        for tile in range(base, base + GROUP):
            place = lists[tile]
            vectors = got[place >> 1, pl.ds(pl.multiple_of((place & 1) * K, K), K), :]
            parts.append(jnp.dot(vectors, tiles[tile], preferred_element_type=f32))
        for tile in range(base, base + GROUP):
            place = lists[count + tile]
            owner = place >> 1
            near = (owner >> 4) * 2 + (owner & 1)
            spot = (near * FARS + ((owner >> 1) & 7)) * 2 + (place & 1)
            where = pl.ds(pl.multiple_of(spot * K, K), K)
            total[where, :] += parts[tile - base]
    message[:, :SLAB, :] = total[...].astype(bf16).reshape(NEARS, SLAB, 128)
    if got.shape[1] > OWN:
        piece = sum_slices(got[:, OWN:, :].reshape(COLUMNS * EXTRA, 128))
        for device in range(NEARS):
            message[device, SLAB:, :] = piece


def near_kernel(got, vectors, message):
    total = got[0, :SLAB, :].astype(f32)
    for device in range(1, NEARS):
        total += got[device, :SLAB, :].astype(f32)
    message[:, OWN : 2 * OWN, :] = total.astype(bf16).reshape(FARS, OWN, 128)
    fill(message, vectors[...].astype(bf16))
    if got.shape[1] > SLAB:
        piece = sum_slices(got[:, SLAB:, :].reshape(NEARS * EXTRA, 128))
        for device in range(FARS):
            message[device, 2 * OWN :, :] = piece


def far_kernel(got, message, column_sums, *piece):
    total = got[0, OWN : 2 * OWN, :].astype(f32)
    for device in range(1, FARS):
        total += got[device, OWN : 2 * OWN, :].astype(f32)
    column_sums[...] = total
    if piece:
        piece[0][...] = sum_slices(got[:, 2 * OWN :, :].reshape(FARS * EXTRA, 128))
    fill(message, got[:, :OWN, :].reshape(SLAB, 128))


def upper_kernel(lists, got, tiles, *refs):
    *piece, message, total = refs
    total[...] = jnp.zeros_like(total)
    count = tiles.shape[0]
    for base in range(0, count, GROUP):
        parts = []
        for tile in range(base, base + GROUP):
            place = lists[count + tile]
            owner = place >> 1
            near = (owner >> 4) * 2 + (owner & 1)
            spot = ((owner >> 1) & 7) * 2 + (place & 1)
            vectors = got[near, pl.ds(pl.multiple_of(spot * K, K), K), :]
            parts.append(jnp.dot(vectors, tiles[tile], preferred_element_type=f32))
        for tile in range(base, base + GROUP):
            where = pl.ds(pl.multiple_of(lists[tile] * K, K), K)
            total[where, :] += parts[tile - base]
    message[:, :OWN, :] = total[...].astype(bf16).reshape(COLUMNS, OWN, 128)
    if piece:
        for device in range(COLUMNS):
            message[device, OWN:, :] = piece[0][...]


def own_part(vectors, diagonal):
    parts = []
    for block in range(OWN // K):
        narrow = vectors[block * K : (block + 1) * K, :].astype(bf16)
        part = dot_t(narrow, diagonal[block], None)
        part += jnp.dot(narrow, diagonal[block], preferred_element_type=f32)
        parts.append(0.5 * part)
    return parts


def image_of(got, column_sums, parts):
    images = []
    for block in range(OWN // K):
        where = slice(block * K, (block + 1) * K)
        total = got[0, where, :].astype(f32)
        for device in range(1, COLUMNS):
            total += got[device, where, :].astype(f32)
        images.append(parts[block] + column_sums[where, :] + total)
    return images


def middle_kernel(got, column_sums, start, part, image, message):
    parts = [part[block * K : (block + 1) * K, :] for block in range(OWN // K)]
    images = image_of(got, column_sums, parts)
    upper = jnp.zeros((K, 2 * K), f32)
    lower = jnp.zeros((K, 2 * K), f32)
    for block in range(OWN // K):
        where = slice(block * K, (block + 1) * K)
        vectors = start[where, :]
        image[where, :] = images[block]
        pair = jnp.concatenate([vectors, images[block]])
        upper += dot_t(vectors, pair)
        lower += dot_t(images[block], pair)
    fill(message, jnp.concatenate(images).astype(bf16))
    grams = jnp.concatenate([upper, lower], axis=1)
    message[:, OWN:, :] = spread_slices(grams).reshape(COLUMNS, EXTRA, 128)


def finish_kernel(
    got, column_sums, start, first, diagonal, basis, image, alpha, beta, message
):
    images = image_of(got, column_sums, own_part(first, diagonal))
    sums = join_slices(got[:, OWN:, :].reshape(COLUMNS * EXTRA, 128))
    work = eliminate(jnp.concatenate([sums, pltpu.roll(sums, 128 - 2 * K, 1)]))
    upper = upper_part(lanes(work[K:], 1))
    inverse = lanes(work[:K], 2)
    weights = pltpu.roll(work[K:], 128 - 2 * K, 1)[:, : 2 * K]
    back = dot(dot_t(upper, inverse), inverse)
    square = jnp.zeros((K, K), f32)
    cross = jnp.zeros((K, K), f32)
    for block in range(OWN // K):
        where = slice(block * K, (block + 1) * K)
        current = dot(weights, jnp.concatenate([start[where, :], first[where, :]]))
        result = dot(weights, jnp.concatenate([first[where, :], images[block]]))
        result -= dot(back, start[where, :])
        basis[where, :] = current
        image[where, :] = result
        square += dot_t(result, result)
        cross += dot_t(current, result)
    packed = pack(square, cross)
    for device in range(message.shape[0]):
        message[device] = packed
    alpha[...] = dot_t(lanes(work[:K], 1), inverse)
    beta[...] = dot_t(inverse, upper)


def plane_kernel(got, message):
    total = got[0]
    for device in range(1, got.shape[0]):
        total += got[device]
    for device in range(message.shape[0]):
        message[device, :, :] = total


def last_kernel(scaling, got, basis, image, alpha_first, beta_first, result, alphas, betas):
    total = got[0]
    for device in range(1, got.shape[0]):
        total += got[device]
    image_gram, alpha_last = unpack(total)
    wide = jnp.zeros((K, 128 - K), f32)
    work = eliminate(jnp.concatenate([image_gram - dot(alpha_last, alpha_last), wide], axis=1))
    upper, inverse = upper_part(work[:, :K]), lanes(work, 1)
    for block in range(OWN // K):
        where = slice(block * K, (block + 1) * K)
        residual = image[where, :] - dot(alpha_last, basis[where, :])
        result[where, :] = dot(inverse, residual) * scaling
    alphas[0] = alpha_first[...]
    alphas[1] = alpha_last
    betas[0] = beta_first[...]
    betas[1] = upper.T


def exchange(message, vectors, tiles, turned, lists):
    extra = message.shape[1] - OWN
    got = swap(message, COLUMN)
    sent = call(
        lower_kernel,
        out((NEARS, SLAB + extra, 128), bf16),
        (lists,),
        (got, tiles),
        (pltpu.VMEM((NEARS * SLAB, 128), f32),),
    )
    got = swap(sent, NEAR)
    sent = call(near_kernel, out((FARS, 2 * OWN + extra, 128), bf16), (), (got, vectors))
    got = swap(sent, FAR)
    outs = [out((NEARS, SLAB, 128), bf16), out((OWN, 128), f32)]
    if extra:
        outs.append(out((extra, 128), bf16))
    sent, column_sums, *piece = call(far_kernel, outs, (), (got,))
    got = swap(sent, NEAR)
    sent = call(
        upper_kernel,
        out((COLUMNS, OWN + extra, 128), bf16),
        (lists,),
        (got, turned, *piece),
        (pltpu.VMEM((COLUMNS * OWN, 128), f32),),
    )
    return swap(sent, COLUMN), column_sums


def local(start_block, tile_values, tile_rows, tile_columns, diagonal_blocks):
    start = start_block.reshape(OWN, 128)
    tiles = tile_values[0, 0]
    *staged, part = call(
        stage_kernel,
        (out(tiles.shape, bf16), out(tiles.shape, bf16), out((OWN, 128), f32)),
        (),
        (tiles, start, diagonal_blocks),
    )
    matrix = (*staged, jnp.concatenate([tile_rows[0, 0], tile_columns[0, 0]]))
    vectors = out((OWN, 128), f32)
    square = out((K, K), f32)
    message = call(prepare_kernel, out((COLUMNS, OWN, 128), bf16), (), (start,))
    got, column_sums = exchange(message, start, *matrix)
    first, message = call(
        middle_kernel,
        (vectors, out((COLUMNS, OWN + EXTRA, 128), bf16)),
        (),
        (got, column_sums, start, part),
    )
    got, column_sums = exchange(message, first, *matrix)
    planes, depths = lax.axis_size(PLANE), lax.axis_size(DEPTH)
    basis, image, alpha_first, beta_first, message = call(
        finish_kernel,
        (vectors, vectors, square, square, out((planes, 1, PACKED), f32)),
        (),
        (got, column_sums, start, first, diagonal_blocks),
    )
    got = swap(message, PLANE)
    message = call(plane_kernel, out((depths, 1, PACKED), f32), (), (got,))
    got = swap(message, DEPTH)
    scaling = math.sqrt(start_block.shape[0] * start_block.shape[2] * planes * depths)
    pair = out((2, K, K), f32)
    result, alphas, betas = call(
        functools.partial(last_kernel, scaling),
        (vectors, pair, pair),
        (),
        (got, basis, image, alpha_first, beta_first),
    )
    return result.reshape(start_block.shape), alphas, betas


def solution(mesh):
    split = Mesh(mesh.devices.reshape(2, FARS, 2, 2, 4, 2), AXES)
    rows = ("x_high", "far", "near")
    owner = P((*COLUMN, *rows), None, None)
    placed = (
        owner,
        P(rows, COLUMN, None, None, None),
        P(rows, COLUMN, None),
        P(rows, COLUMN, None),
        owner,
    )
    return jax.shard_map(
        local,
        mesh=split,
        in_specs=placed,
        out_specs=(owner, P(), P()),
        check_vma=False,
    )
```
